32 devices in a mesh: expert: 16 (over z, y, x), token: 2 (over core).
Axes of the slice: x: 2, y: 2, z: 4, core: 2. Of those that a mesh axis runs over, the one named last changes fastest.
Arguments:
- tokens: bfloat16 [1024, 3584], P('expert', 'token'), may hold values from -6 to 6
- routes: int32 [1024, 8], P('expert'), may hold values from 0 to 15, all different within a row; in each aligned block of 64 rows (0 to 63, 64 to 127, ...) at most 64 rows name the same one
- mixing: float32 [1024, 8], P('expert'), may hold values from 0.05 to 1
- gate_weight: bfloat16 [16, 3584, 1024], P('expert', None, 'token'), may hold values from -0.09375 to 0.09375
- up_weight: bfloat16 [16, 3584, 1024], P('expert', None, 'token'), may hold values from -0.09375 to 0.09375
- down_weight: bfloat16 [16, 1024, 3584], P('expert', None, 'token'), may hold values from -0.1875 to 0.1875
Outputs:
- mixed: bfloat16 [1024, 3584], P('expert', 'token')
- hessian: float32 [16, 1024, 1024], P('expert', 'token')
The draws below stay inside these ranges and needn't reach their ends.
Inputs may be any that keep to these rules, and one draw needn't show every extreme that they name: `routes`: each row names 8 different experts; among the 64 rows of one device no expert is named by more than 64 rows, and on some device an expert is named by exactly 64 rows; every expert is named by some row.
All inputs are finite; a program needn't handle non-finite values.
Results may differ from the reference program's by a relative error of at most 0.0058.
Values may be sent and summed in bfloat16 or wider, within the bound.
A program may use at most 128 MiB of HBM per device.

```python
import math
import jax
import jax.numpy as jnp
import numpy as np
from jax import lax

D = 3584
FF = 1024
TOPK = 8
TOK_E = 64
EXPERTS = 16
TOKENS = 1024
CAP = 64
N_EXPERT = 16


def shard_levels(stream_key, shape, pieces, least, largest):
    gain = 1.0
    for dim, shards_of in pieces:
        draws = jax.random.uniform(jax.random.fold_in(jax.random.fold_in(stream_key, 6), dim), (shards_of,), jnp.float32, least / len(pieces), largest / len(pieces))
        gain = gain * jnp.repeat(jnp.exp(draws), shape[dim] // shards_of).reshape((-1,) + (1,) * (len(shape) - 1 - dim))
    return gain


def shared_out(own_key, own, number, rows, amount, top, reach, slope):
    ranking = jax.random.permutation(own_key, amount)
    heavy_load, common = load_shares(amount, rows * top, reach, slope, True), load_shares(amount, rows * top, reach, slope, False)
    places = jnp.arange(amount)

    def named(sizes, rotation):
        used = int((sizes > 0).sum())
        fixed = max(1, used // 4)
        shifted = fixed + (places - fixed + rotation * (used - fixed)) % max(1, amount - fixed)
        return jnp.zeros((amount,), jnp.int32).at[ranking[jnp.where(places < fixed, places, shifted)]].set(jnp.asarray(sizes, jnp.int32))

    sizes = jnp.where(number % 4 == 0, named(heavy_load, number // 4), named(common, number - number // 4 - 1))
    mixed = jax.random.permutation(jax.random.fold_in(own, 3), amount)
    giver, taker = mixed[0:amount // 2 * 2:2], mixed[1:amount // 2 * 2:2]
    margin = jnp.minimum(sizes[giver] - 1, reach - sizes[taker]) // 2
    margin = jnp.where((giver == ranking[0]) | (taker == ranking[0]) | (sizes[taker] == 0), 0, jnp.maximum(margin, 0))
    shifted = jax.random.randint(jax.random.fold_in(own, 4), (amount // 2,), 0, 1 << 20) % (margin + 1)
    sizes = sizes.at[giver].add(-shifted).at[taker].add(shifted)
    members = jnp.searchsorted(jnp.cumsum(sizes), jnp.arange(rows * top), side="right").astype(jnp.int32)
    table = members.reshape(top, rows).T
    table = table[jax.random.permutation(jax.random.fold_in(own, 1), rows)]
    rotation = jax.random.randint(jax.random.fold_in(own, 2), (rows, 1), 0, top)
    return jnp.take_along_axis(table, (jnp.arange(top)[None, :] + rotation) % top, axis=1)


def load_shares(number_of, total, bound, lean, full):
    portions = [(1 << 20) // math.isqrt(rank ** lean) + 1 for rank in range(1, number_of + 1)]
    largest = bound if full else min(bound, max(-(-total // number_of), total * portions[0] // sum(portions)))
    least = 1 if total - largest >= number_of - 1 else 0
    given, surplus = [largest] + [least] * (number_of - 1), total - largest - least * (number_of - 1)
    while surplus > 0:
        candidates = [i for i in range(1, number_of) if given[i] < largest] or [i for i in range(1, number_of) if given[i] < bound]
        whole, remaining = sum([portions[i] for i in candidates]), surplus
        for i in candidates:
            addition = min(bound - given[i], max(1, remaining * portions[i] // whole), surplus)
            given[i] = given[i] + addition
            surplus = surplus - addition
    return np.array(given)


def scatter_about(own_key, dims, deviation, limit, split=(), kind=jnp.bfloat16):
    values = deviation * jax.random.normal(own_key, dims, jnp.float32)
    if split:
        values = values * shard_levels(own_key, dims, split, -0.22, 0.18)
    return jnp.clip(values, -limit, limit).astype(kind)


def setup_inputs(seed: int = 0) -> dict:
    splits = jax.random.split(jax.random.key(seed), 7)
    tokens = scatter_about(splits[0], (TOKENS, D), 1.0, 6.0, ((0, 16), (1, 2)))
    routes_keys = jax.random.split(jax.random.fold_in(splits[1], 1), TOKENS // TOK_E)
    routes_turns = jax.random.permutation(jax.random.fold_in(splits[1], 3), TOKENS // TOK_E)
    routes = jax.vmap(lambda own, number: shared_out(jax.random.fold_in(splits[1], 2), own, number, TOK_E, EXPERTS, TOPK, CAP, 2))(routes_keys, routes_turns).reshape((TOKENS, TOPK))
    mixing = jnp.clip(jnp.exp(math.log(1.0) - 2.9957323 * jax.random.uniform(splits[2], (TOKENS, TOPK), jnp.float32) ** shard_levels(splits[2], (TOKENS, TOPK), ((0, 16),), -0.2, 0.2)), 0.05, 1.0)
    gate_weight = scatter_about(splits[3], (EXPERTS, D, FF), D ** -0.5, 0.09375, ((0, 16), (2, 2)))
    up_weight = scatter_about(splits[4], (EXPERTS, D, FF), D ** -0.5, 0.09375, ((0, 16), (2, 2)))
    down_weight = scatter_about(splits[5], (EXPERTS, FF, D), FF ** -0.5, 0.1875, ((0, 16), (2, 2)))
    return {"tokens": tokens, "routes": routes, "mixing": mixing, "gate_weight": gate_weight, "up_weight": up_weight, "down_weight": down_weight}


def reference(tokens, routes, mixing, gate_weight, up_weight, down_weight):
    tok_count = routes.shape[0]
    top_count = routes.shape[1]
    expert_count = gate_weight.shape[0]
    most_rows = N_EXPERT * CAP
    flat_ids = routes.reshape(-1).astype(jnp.int32)
    order = jnp.argsort(flat_ids, stable=True).astype(jnp.int32)
    counts = jnp.sum((flat_ids[:, None] == jnp.arange(expert_count, dtype=jnp.int32)[None, :]).astype(jnp.int32), 0)
    offsets = (jnp.cumsum(counts) - counts).astype(jnp.int32)
    padded = jnp.concatenate([order, jnp.zeros((most_rows,), jnp.int32)])

    def one_expert(index):
        picked = lax.dynamic_slice(padded, (offsets[index],), (most_rows,))
        valid = jnp.arange(most_rows, dtype=jnp.int32) < counts[index]
        rows = jnp.where(valid[:, None], tokens[picked // top_count], jnp.zeros((), tokens.dtype))
        gate = jnp.dot(rows, gate_weight[index], preferred_element_type=jnp.float32)
        upper = jnp.dot(rows, up_weight[index], preferred_element_type=jnp.float32)
        hidden = (jax.nn.silu(gate) * upper).astype(jnp.bfloat16)
        result = jnp.dot(hidden, down_weight[index], preferred_element_type=jnp.float32).astype(jnp.bfloat16)
        gram = jnp.dot(hidden.T, hidden, preferred_element_type=jnp.float32)
        return result, (2.0 / counts[index].astype(jnp.float32)) * gram

    outputs, hessian = lax.map(one_expert, jnp.arange(expert_count, dtype=jnp.int32))
    inverse = jnp.zeros(flat_ids.shape, jnp.int32).at[order].set(jnp.arange(flat_ids.shape[0], dtype=jnp.int32))
    position = (inverse - offsets[flat_ids]).astype(jnp.int32)
    gathered = outputs[flat_ids, position].reshape(tok_count, top_count, -1)
    mixed = jnp.sum(gathered.astype(jnp.float32) * mixing[:, :, None], 1).astype(jnp.bfloat16)
    return mixed, hessian
```

```python
import jax
import jax.numpy as jnp
from jax import lax
from jax.sharding import PartitionSpec as P


def dispatch(tokens, routes, mixing, gate_weight, up_weight, down_weight):
    tok_rows = tokens.shape[0]
    feat_width = tokens.shape[1]
    top_count = routes.shape[1]
    expert_count = lax.axis_size("expert")
    capacity = 2 * tok_rows * top_count // expert_count
    slot_total = expert_count * capacity
    flat_ids = routes.reshape(-1)
    chosen = (flat_ids[:, None] == jnp.arange(expert_count, dtype=jnp.int32)[None, :]).astype(
        jnp.int32
    )
    ranks = jnp.cumsum(chosen, axis=0) - chosen
    slots = jnp.sum(ranks * chosen, axis=1)
    counts = jnp.sum(chosen, axis=0)
    target = flat_ids * capacity + slots
    placing = (target[:, None] == jnp.arange(slot_total, dtype=jnp.int32)[None, :]).astype(
        jnp.bfloat16
    )
    placing = jnp.sum(placing.reshape(tok_rows, top_count, slot_total), axis=1)
    outgoing = lax.dot_general(
        placing, tokens, (((0,), (0,)), ((), ())), preferred_element_type=jnp.float32
    )
    outgoing = outgoing.astype(jnp.bfloat16).reshape(expert_count, capacity, feat_width)
    received, got_counts = (
        lax.all_to_all(outgoing, "expert", split_axis=0, concat_axis=0, tiled=True),
        lax.all_to_all(
            counts.astype(jnp.bfloat16), "expert", split_axis=0, concat_axis=0, tiled=True
        ),
    )
    rows_in = received.reshape(slot_total, feat_width)
    row_total = jnp.sum(got_counts.astype(jnp.float32))
    gate_local = gate_weight[0]
    up_local = up_weight[0]
    piece = lax.all_gather(rows_in, "token", axis=1, tiled=True)
    gate = jnp.dot(piece, gate_local, preferred_element_type=jnp.float32)
    upper = jnp.dot(piece, up_local, preferred_element_type=jnp.float32)
    hidden = (jax.nn.silu(gate) * upper).astype(jnp.bfloat16)
    down_local = down_weight[0]
    piece = lax.all_gather(hidden, "token", axis=1, tiled=True)
    out_sum = jnp.dot(piece, down_local, preferred_element_type=jnp.float32)
    outer = lax.dot_general(
        hidden, piece, (((0,), (0,)), ((), ())), preferred_element_type=jnp.float32
    )
    gram = outer
    out_sum, gram = (out_sum, gram)
    hessian = (2.0 / row_total * gram)[None]
    expert_out = out_sum.astype(jnp.bfloat16).reshape(expert_count, capacity, feat_width)
    returned = lax.all_to_all(expert_out, "expert", split_axis=0, concat_axis=0, tiled=True)
    picked = returned.reshape(slot_total, feat_width)[target]
    picked = picked.reshape(tok_rows, top_count, feat_width).astype(jnp.float32)
    mixed = jnp.sum(picked * mixing[:, :, None], axis=1).astype(jnp.bfloat16)
    return (mixed, hessian)


def dense(tokens, routes, mixing, gate_weight, up_weight, down_weight):
    expert_count = lax.axis_size("expert")
    me = lax.axis_index("expert")
    ids = jnp.arange(expert_count, dtype=jnp.int32)
    share = jnp.sum(
        jnp.where(routes[:, :, None] == ids[None, None, :], mixing[:, :, None], 0.0), axis=1
    )
    shares = lax.all_gather(share, "expert", axis=0, tiled=True)
    mine = jnp.sum(jnp.where(ids[None, :] == me, shares, 0.0), axis=1, keepdims=True)
    row_total = jnp.sum((mine > 0).astype(jnp.float32))
    rows = lax.all_gather(tokens, "expert", axis=0, tiled=True)
    rows = lax.all_gather(rows, "token", axis=1, tiled=True)
    gate = jnp.dot(rows, gate_weight[0], preferred_element_type=jnp.float32)
    upper = jnp.dot(rows, up_weight[0], preferred_element_type=jnp.float32)
    hidden = jnp.where(mine > 0, jax.nn.silu(gate) * upper, 0.0).astype(jnp.bfloat16)
    piece = lax.all_gather(hidden, "token", axis=1, tiled=True)
    part = jnp.dot(piece, down_weight[0], preferred_element_type=jnp.float32)
    part = (part * mine).astype(jnp.bfloat16)
    gram = lax.dot_general(
        hidden, piece, (((0,), (0,)), ((), ())), preferred_element_type=jnp.float32
    )
    hessian = (2.0 / row_total * gram)[None]
    mixed = lax.psum_scatter(part, "expert", scatter_dimension=0, tiled=True)
    return (mixed, hessian)


def shards(tokens, routes, mixing, gate_weight, up_weight, down_weight):
    tok_rows, top_count = routes.shape
    expert_count = lax.axis_size("expert")
    if 2 * top_count >= expert_count:
        return dense(tokens, routes, mixing, gate_weight, up_weight, down_weight)
    return dispatch(tokens, routes, mixing, gate_weight, up_weight, down_weight)


def solution(mesh):
    placed = (
        P("expert", "token"),
        P("expert", None),
        P("expert", None),
        P("expert", None, "token"),
        P("expert", None, "token"),
        P("expert", None, "token"),
    )
    return jax.shard_map(
        shards,
        mesh=mesh,
        in_specs=placed,
        out_specs=(P("expert", "token"), P("expert", "token", None)),
        check_vma=False,
    )
```

```python
import functools
import math

import jax
import jax.numpy as jnp
from jax import lax
from jax.experimental import pallas as pl
from jax.experimental.pallas import tpu as pltpu
from jax.sharding import PartitionSpec as P

MESH = pl.DeviceIdType.MESH


def dispatch(tokens, routes, mixing, gate_weight, up_weight, down_weight):
    tok_rows = tokens.shape[0]
    feat_width = tokens.shape[1]
    top_count = routes.shape[1]
    expert_count = lax.axis_size("expert")
    capacity = 2 * tok_rows * top_count // expert_count
    slot_total = expert_count * capacity
    flat_ids = routes.reshape(-1)
    chosen = (flat_ids[:, None] == jnp.arange(expert_count, dtype=jnp.int32)[None, :]).astype(
        jnp.int32
    )
    ranks = jnp.cumsum(chosen, axis=0) - chosen
    slots = jnp.sum(ranks * chosen, axis=1)
    counts = jnp.sum(chosen, axis=0)
    target = flat_ids * capacity + slots
    placing = (target[:, None] == jnp.arange(slot_total, dtype=jnp.int32)[None, :]).astype(
        jnp.bfloat16
    )
    placing = jnp.sum(placing.reshape(tok_rows, top_count, slot_total), axis=1)
    outgoing = lax.dot_general(
        placing, tokens, (((0,), (0,)), ((), ())), preferred_element_type=jnp.float32
    )
    outgoing = outgoing.astype(jnp.bfloat16).reshape(expert_count, capacity, feat_width)
    received, got_counts = (
        lax.all_to_all(outgoing, "expert", split_axis=0, concat_axis=0, tiled=True),
        lax.all_to_all(
            counts.astype(jnp.bfloat16), "expert", split_axis=0, concat_axis=0, tiled=True
        ),
    )
    rows_in = received.reshape(slot_total, feat_width)
    row_total = jnp.sum(got_counts.astype(jnp.float32))
    gate_local = gate_weight[0]
    up_local = up_weight[0]
    piece = lax.all_gather(rows_in, "token", axis=1, tiled=True)
    gate = jnp.dot(piece, gate_local, preferred_element_type=jnp.float32)
    upper = jnp.dot(piece, up_local, preferred_element_type=jnp.float32)
    hidden = (jax.nn.silu(gate) * upper).astype(jnp.bfloat16)
    down_local = down_weight[0]
    piece = lax.all_gather(hidden, "token", axis=1, tiled=True)
    out_sum = jnp.dot(piece, down_local, preferred_element_type=jnp.float32)
    outer = lax.dot_general(
        hidden, piece, (((0,), (0,)), ((), ())), preferred_element_type=jnp.float32
    )
    gram = outer
    out_sum, gram = (out_sum, gram)
    hessian = (2.0 / row_total * gram)[None]
    expert_out = out_sum.astype(jnp.bfloat16).reshape(expert_count, capacity, feat_width)
    returned = lax.all_to_all(expert_out, "expert", split_axis=0, concat_axis=0, tiled=True)
    picked = returned.reshape(slot_total, feat_width)[target]
    picked = picked.reshape(tok_rows, top_count, feat_width).astype(jnp.float32)
    mixed = jnp.sum(picked * mixing[:, :, None], axis=1).astype(jnp.bfloat16)
    return (mixed, hessian)


def exchange(
    side,
    layers,
    tokens_hbm,
    routes_ref,
    mixing_ref,
    gate_hbm,
    up_hbm,
    down_hbm,
    mixed_ref,
    hess_hbm,
    tok,
    table,
    weight,
    gate_v,
    up_v,
    down_v,
    hid,
    part,
    in_b,
    in_a,
    in_z,
    hess_v,
    local_sem,
    tok_send,
    tok_recv,
    tab_send,
    tab_recv,
    pair_send,
    pair_recv,
    hid_send,
    hid_recv,
    back_send,
    back_recv,
):
    groups = side * side
    rows, width = mixed_ref.shape
    half = gate_v.shape[2]
    me = lax.axis_index("expert")
    core = lax.axis_index("token")
    z, y, x = me // groups, (me // side) % side, me % side
    stride_a = jnp.where(core == 0, side, 1)
    stride_b = jnp.where(core == 0, 1, side)
    pos_a = jnp.where(core == 0, y, x)
    pos_b = jnp.where(core == 0, x, y)

    def peer_z(step):
        return me + ((z + step) % layers - z) * groups

    def peer_a(step):
        return me + ((pos_a + step) % side - pos_a) * stride_a

    def peer_b(step):
        return me + ((pos_b + step) % side - pos_b) * stride_b

    def slot(dz, da, db):
        return (da * stride_a + db * stride_b) * layers + dz

    def label(dz, da, db):
        return (da * side + db) * layers + dz

    def remote(src, dst, send, recv, to, to_core=None):
        return pltpu.make_async_remote_copy(
            src_ref=src,
            dst_ref=dst,
            send_sem=send,
            recv_sem=recv,
            device_id=(to, core if to_core is None else to_core),
            device_id_type=MESH,
        )

    def forward(dz, da, db):
        if db:
            source, to = slot(dz, da, 0), peer_b(db)
        elif da:
            source, to = slot(dz, 0, 0), peer_a(da)
        else:
            source, to = slot(0, 0, 0), peer_z(dz)
        name = label(dz, da, db)
        here = slot(dz, da, db)
        return (
            remote(table.at[source], table.at[here], tab_send.at[name], tab_recv.at[name], to),
            remote(
                tok.at[core, source],
                tok.at[core, here],
                tok_send.at[name],
                tok_recv.at[name],
                to,
            ),
        )

    def start(copies):
        for copy in copies:
            copy.start()

    def arrive(copies):
        for copy in copies:
            copy.wait_recv()

    def across(where):
        return remote(
            tok.at[core, where],
            tok.at[core, where],
            pair_send.at[where],
            pair_recv.at[where],
            me,
            1 - core,
        )

    def from_pair(where):
        return remote(
            tok.at[1 - core, where],
            tok.at[1 - core, where],
            pair_send.at[where],
            pair_recv.at[where],
            me,
            1 - core,
        )

    loads = [
        pltpu.make_async_copy(tokens_hbm, tok.at[core, 0], local_sem.at[0]),
        pltpu.make_async_copy(gate_hbm, gate_v, local_sem.at[1]),
        pltpu.make_async_copy(up_hbm, up_v, local_sem.at[2]),
        pltpu.make_async_copy(down_hbm, down_v, local_sem.at[3]),
    ]
    start(loads)
    barrier = pltpu.get_barrier_semaphore()
    partners = [(peer_z(d), core) for d in range(1, layers)]
    partners += [(peer_a(d), core) for d in range(1, side)]
    partners += [(peer_b(d), core) for d in range(1, side)]
    partners += [(me, 1 - core)]
    for partner in partners:
        pl.semaphore_signal(barrier, inc=1, device_id=partner, device_id_type=MESH)
    named = lax.broadcasted_iota(jnp.int32, (table.shape[1], rows), 0)
    shares = jnp.zeros((table.shape[1], rows), jnp.float32)
    for k in range(routes_ref.shape[0]):
        shares += jnp.where(routes_ref[k : k + 1, :] == named, mixing_ref[k : k + 1, :], 0.0)
    table[0, :, 0:rows] = shares
    loads[0].wait()
    pl.semaphore_wait(barrier, len(partners))

    for dz in range(1, layers):
        start(forward(dz, 0, 0))
    for d in range(1, side):
        start(forward(0, d, 0))
        start(forward(0, 0, d))
    across(slot(0, 0, 0)).start()
    for dz in range(1, layers):
        arrive(forward(dz, 0, 0))
        for d in range(1, side):
            start(forward(dz, d, 0))
            start(forward(dz, 0, d))
        across(slot(dz, 0, 0)).start()
    for da in range(1, side):
        for dz in range(layers):
            arrive(forward(dz, da, 0))
            for db in range(1, side):
                start(forward(dz, da, db))
            across(slot(dz, da, 0)).start()

    tall = layers * rows
    tile = min(256, half)
    diagonal = lax.broadcasted_iota(jnp.int32, (rows, rows), 0) == lax.broadcasted_iota(
        jnp.int32, (rows, rows), 1
    )

    def up_project(g):
        first = g * layers
        span = pl.ds(first, layers)
        for i in range(layers):
            from_pair(first + i).wait_recv()
            mine = table[first + i, pl.ds(me, 1), 0:rows]
            column = jnp.sum(jnp.where(diagonal, mine, 0.0), axis=1, keepdims=True)
            weight[first + i] = jnp.broadcast_to(column, weight.shape[1:])

        @pl.loop(0, half // tile)
        def _(j):
            cols = pl.ds(pl.multiple_of(j * tile, tile), tile)
            left = tok[0, span].reshape(tall, width)
            right = tok[1, span].reshape(tall, width)
            gate = jnp.dot(left, gate_v[0, :, cols], preferred_element_type=jnp.float32)
            gate += jnp.dot(right, gate_v[1, :, cols], preferred_element_type=jnp.float32)
            upper = jnp.dot(left, up_v[0, :, cols], preferred_element_type=jnp.float32)
            upper += jnp.dot(right, up_v[1, :, cols], preferred_element_type=jnp.float32)
            chosen = weight[span].reshape(tall, weight.shape[2])[:, 0:1] > 0
            value = gate / (1.0 + jnp.exp(-gate)) * upper
            value = jnp.where(chosen, value, 0.0).astype(jnp.bfloat16)
            hid[core, span, :, cols] = value.reshape(layers, rows, tile)

        hidden_copy(g).start()

    def hidden_copy(g):
        span = pl.ds(g * layers, layers)
        return remote(
            hid.at[core, span],
            hid.at[core, span],
            hid_send.at[g],
            hid_recv.at[g],
            me,
            1 - core,
        )

    def hidden_from_pair(g):
        span = pl.ds(g * layers, layers)
        return remote(
            hid.at[1 - core, span],
            hid.at[1 - core, span],
            hid_send.at[g],
            hid_recv.at[g],
            me,
            1 - core,
        )

    def down_project(g):
        span = pl.ds(g * layers, layers)
        hidden_from_pair(g).wait_recv()

        @pl.loop(0, width // tile)
        def _(j):
            cols = pl.ds(pl.multiple_of(j * tile, tile), tile)
            left = hid[0, span].reshape(tall, half)
            right = hid[1, span].reshape(tall, half)
            out = jnp.dot(left, down_v[0, :, cols], preferred_element_type=jnp.float32)
            out += jnp.dot(right, down_v[1, :, cols], preferred_element_type=jnp.float32)
            out *= weight[span].reshape(tall, weight.shape[2])[:, 0:1]
            part[span, :, cols] = out.astype(jnp.bfloat16).reshape(layers, rows, tile)

    def back(dz, da, db):
        name = label(dz, da, db)
        source = part.at[slot(dz, da, db)]
        if db:
            target, to = in_b.at[db - 1, da * layers + dz], peer_b(side - db)
        elif da:
            target, to = in_a.at[da - 1, dz], peer_a(side - da)
        else:
            target, to = in_z.at[dz - 1], peer_z(layers - dz)
        return remote(source, target, back_send.at[name], back_recv.at[name], to)

    def summed(dz, da):
        total = part[slot(dz, da, 0)].astype(jnp.float32)
        for db in range(1, side):
            back(dz, da, db).wait_recv()
            total += in_b[db - 1, da * layers + dz].astype(jnp.float32)
        if da == 0:
            for d in range(1, side):
                back(dz, d, 0).wait_recv()
                total += in_a[d - 1, dz].astype(jnp.float32)
        return total

    for load in loads[1:]:
        load.wait()
    up_project(0)
    for db in range(1, side):
        for dz in range(layers):
            arrive(forward(dz, 0, db))
            across(slot(dz, 0, db)).start()
    down_project(0)
    edge = [g for g in range(1, groups) if g // side == 0 or g % side == 0]
    inner = [g for g in range(1, groups) if g not in edge]
    for g in edge:
        up_project(g)
    for da in range(1, side):
        for db in range(1, side):
            for dz in range(layers):
                arrive(forward(dz, da, db))
                across(slot(dz, da, db)).start()
    for g in edge:
        down_project(g)
    for db in range(1, side):
        for dz in range(layers):
            back(dz, 0, db).start()
    for g in inner:
        up_project(g)
    for g in inner:
        down_project(g)
    for da in range(1, side):
        for db in range(1, side):
            for dz in range(layers):
                back(dz, da, db).start()

    named_rows = jnp.zeros((rows, weight.shape[2]), jnp.float32)
    for s in range(weight.shape[0]):
        named_rows += (weight[s] > 0).astype(jnp.float32)
    count = jnp.sum(named_rows, axis=0, keepdims=True)[:, 0:1]
    scale = 2.0 / count
    every = weight.shape[0] * rows
    for h in range(2):

        @pl.loop(0, half // tile)
        def _(j):
            cols = pl.ds(pl.multiple_of(j * tile, tile), tile)
            gram = lax.dot_general(
                hid[core, :, :, cols].reshape(every, tile),
                hid[h].reshape(every, half),
                (((0,), (0,)), ((), ())),
                preferred_element_type=jnp.float32,
            )
            hess_v[cols, pl.ds(h * half, half)] = gram * scale

    store = pltpu.make_async_copy(hess_v, hess_hbm, local_sem.at[0])
    store.start()

    for da in range(1, side):
        for dz in range(layers):
            part[slot(dz, da, 0)] = summed(dz, da).astype(jnp.bfloat16)
            back(dz, da, 0).start()
    for dz in range(1, layers):
        part[dz] = summed(dz, 0).astype(jnp.bfloat16)
        back(dz, 0, 0).start()
    total = summed(0, 0)
    for dz in range(1, layers):
        back(dz, 0, 0).wait_recv()
        total += in_z[dz - 1].astype(jnp.float32)
    mixed_ref[...] = total.astype(jnp.bfloat16)

    store.wait()
    for da in range(side):
        for db in range(side):
            for dz in range(layers):
                across(slot(dz, da, db)).wait_send()
                if dz or da or db:
                    for copy in forward(dz, da, db):
                        copy.wait_send()
                    back(dz, da, db).wait_send()
    for g in range(groups):
        hidden_copy(g).wait_send()


def gathered(tokens, routes, mixing, gate_weight, up_weight, down_weight):
    count = lax.axis_size("expert")
    side = math.isqrt(count // 4)
    layers = count // (side * side)
    rows, width = tokens.shape
    depth, half = gate_weight.shape[1:]
    lanes = -(-rows // 128) * 128
    bf16, f32 = jnp.bfloat16, jnp.float32
    dma = pltpu.SemaphoreType.DMA
    hbm = pl.BlockSpec(memory_space=pl.ANY)
    vmem = pl.BlockSpec(memory_space=pltpu.VMEM)
    flops = 2 * count * rows * (2 * depth * half + 2 * half * width + 2 * half * half)
    mixed, hessian = pl.pallas_call(
        functools.partial(exchange, side, layers),
        out_shape=(
            jax.ShapeDtypeStruct((rows, width), bf16),
            jax.ShapeDtypeStruct((half, 2 * half), f32),
        ),
        in_specs=[hbm, vmem, vmem, hbm, hbm, hbm],
        out_specs=(vmem, hbm),
        scratch_shapes=[
            pltpu.VMEM((2, count, rows, width), bf16),
            pltpu.VMEM((count, count, lanes), f32),
            pltpu.VMEM((count, rows, 128), f32),
            pltpu.VMEM((2, width, half), bf16),
            pltpu.VMEM((2, width, half), bf16),
            pltpu.VMEM((2, half, width), bf16),
            pltpu.VMEM((2, count, rows, half), bf16),
            pltpu.VMEM((count, rows, width), bf16),
            pltpu.VMEM((side - 1, side * layers, rows, width), bf16),
            pltpu.VMEM((side - 1, layers, rows, width), bf16),
            pltpu.VMEM((layers - 1, rows, width), bf16),
            pltpu.VMEM((half, 2 * half), f32),
            dma((4,)),
            dma((count,)),
            dma((count,)),
            dma((count,)),
            dma((count,)),
            dma((count,)),
            dma((count,)),
            dma((side * side,)),
            dma((side * side,)),
            dma((count,)),
            dma((count,)),
        ],
        compiler_params=pltpu.CompilerParams(
            collective_id=0, has_side_effects=True, vmem_limit_bytes=60 * 2**20
        ),
        cost_estimate=pl.CostEstimate(
            flops=flops,
            bytes_accessed=2 * (2 * depth * half + 2 * half * width),
            transcendentals=count * rows * half,
        ),
    )(
        tokens,
        routes.T,
        mixing.T,
        gate_weight.reshape(2, width, half),
        up_weight.reshape(2, width, half),
        down_weight.reshape(2, half, width),
    )
    return (mixed, hessian[None])


def shards(tokens, routes, mixing, gate_weight, up_weight, down_weight):
    expert_count = lax.axis_size("expert")
    if 2 * routes.shape[1] >= expert_count:
        return gathered(tokens, routes, mixing, gate_weight, up_weight, down_weight)
    return dispatch(tokens, routes, mixing, gate_weight, up_weight, down_weight)


def solution(mesh):
    placed = (
        P("expert", "token"),
        P("expert", None),
        P("expert", None),
        P("expert", None, "token"),
        P("expert", None, "token"),
        P("expert", None, "token"),
    )
    return jax.shard_map(
        shards,
        mesh=mesh,
        in_specs=placed,
        out_specs=(P("expert", "token"), P("expert", "token", None)),
        check_vma=False,
    )
```

```python
import functools
import math

import jax
import jax.numpy as jnp
from jax import lax
from jax.experimental import pallas as pl
from jax.experimental.pallas import tpu as pltpu
from jax.sharding import PartitionSpec as P

MESH = pl.DeviceIdType.MESH


def dispatch(tokens, routes, mixing, gate_weight, up_weight, down_weight):
    tok_rows = tokens.shape[0]
    feat_width = tokens.shape[1]
    top_count = routes.shape[1]
    expert_count = lax.axis_size("expert")
    capacity = 2 * tok_rows * top_count // expert_count
    slot_total = expert_count * capacity
    flat_ids = routes.reshape(-1)
    chosen = (flat_ids[:, None] == jnp.arange(expert_count, dtype=jnp.int32)[None, :]).astype(
        jnp.int32
    )
    ranks = jnp.cumsum(chosen, axis=0) - chosen
    slots = jnp.sum(ranks * chosen, axis=1)
    counts = jnp.sum(chosen, axis=0)
    target = flat_ids * capacity + slots
    placing = (target[:, None] == jnp.arange(slot_total, dtype=jnp.int32)[None, :]).astype(
        jnp.bfloat16
    )
    placing = jnp.sum(placing.reshape(tok_rows, top_count, slot_total), axis=1)
    outgoing = lax.dot_general(
        placing, tokens, (((0,), (0,)), ((), ())), preferred_element_type=jnp.float32
    )
    outgoing = outgoing.astype(jnp.bfloat16).reshape(expert_count, capacity, feat_width)
    received, got_counts = (
        lax.all_to_all(outgoing, "expert", split_axis=0, concat_axis=0, tiled=True),
        lax.all_to_all(
            counts.astype(jnp.bfloat16), "expert", split_axis=0, concat_axis=0, tiled=True
        ),
    )
    rows_in = received.reshape(slot_total, feat_width)
    row_total = jnp.sum(got_counts.astype(jnp.float32))
    gate_local = gate_weight[0]
    up_local = up_weight[0]
    piece = lax.all_gather(rows_in, "token", axis=1, tiled=True)
    gate = jnp.dot(piece, gate_local, preferred_element_type=jnp.float32)
    upper = jnp.dot(piece, up_local, preferred_element_type=jnp.float32)
    hidden = (jax.nn.silu(gate) * upper).astype(jnp.bfloat16)
    down_local = down_weight[0]
    piece = lax.all_gather(hidden, "token", axis=1, tiled=True)
    out_sum = jnp.dot(piece, down_local, preferred_element_type=jnp.float32)
    outer = lax.dot_general(
        hidden, piece, (((0,), (0,)), ((), ())), preferred_element_type=jnp.float32
    )
    gram = outer
    out_sum, gram = (out_sum, gram)
    hessian = (2.0 / row_total * gram)[None]
    expert_out = out_sum.astype(jnp.bfloat16).reshape(expert_count, capacity, feat_width)
    returned = lax.all_to_all(expert_out, "expert", split_axis=0, concat_axis=0, tiled=True)
    picked = returned.reshape(slot_total, feat_width)[target]
    picked = picked.reshape(tok_rows, top_count, feat_width).astype(jnp.float32)
    mixed = jnp.sum(picked * mixing[:, :, None], axis=1).astype(jnp.bfloat16)
    return (mixed, hessian)


def exchange(
    side,
    layers,
    tokens_hbm,
    routes_ref,
    mixing_ref,
    gate_hbm,
    up_hbm,
    down_hbm,
    mixed_ref,
    hess_hbm,
    tok,
    table,
    weight,
    gate_v,
    up_v,
    down_v,
    hid,
    part,
    in_b,
    in_a,
    in_z,
    hess_v,
    local_sem,
    tok_send,
    tok_recv,
    tab_send,
    tab_recv,
    pair_send,
    pair_recv,
    hid_send,
    hid_recv,
    back_send,
    back_recv,
    chain_send,
):
    groups = side * side
    rows, width = mixed_ref.shape
    half = gate_v.shape[2]
    me = lax.axis_index("expert")
    core = lax.axis_index("token")
    z, y, x = me // groups, (me // side) % side, me % side
    stride_a = jnp.where(core == 0, side, 1)
    stride_b = jnp.where(core == 0, 1, side)
    pos_a = jnp.where(core == 0, y, x)
    pos_b = jnp.where(core == 0, x, y)

    def peer_z(step):
        return me + ((z + step) % layers - z) * groups

    def peer_a(step):
        return me + ((pos_a + step) % side - pos_a) * stride_a

    def peer_b(step):
        return me + ((pos_b + step) % side - pos_b) * stride_b

    def slot(dz, da, db):
        return (da * stride_a + db * stride_b) * layers + dz

    def label(dz, da, db):
        return (da * side + db) * layers + dz

    def remote(src, dst, send, recv, to, to_core=None):
        return pltpu.make_async_remote_copy(
            src_ref=src,
            dst_ref=dst,
            send_sem=send,
            recv_sem=recv,
            device_id=(to, core if to_core is None else to_core),
            device_id_type=MESH,
        )

    def forward(dz, da, db):
        if db:
            source, to = slot(dz, da, 0), peer_b(db)
        elif da:
            source, to = slot(dz, 0, 0), peer_a(da)
        else:
            source, to = slot(0, 0, 0), peer_z(dz)
        name = label(dz, da, db)
        here = slot(dz, da, db)
        return (
            remote(table.at[source], table.at[here], tab_send.at[name], tab_recv.at[name], to),
            remote(
                tok.at[core, source],
                tok.at[core, here],
                tok_send.at[name],
                tok_recv.at[name],
                to,
            ),
        )

    def start(copies):
        for copy in copies:
            copy.start()

    def arrive(copies):
        for copy in copies:
            copy.wait_recv()

    def across(where):
        return remote(
            tok.at[core, where],
            tok.at[core, where],
            pair_send.at[where],
            pair_recv.at[where],
            me,
            1 - core,
        )

    def from_pair(where):
        return remote(
            tok.at[1 - core, where],
            tok.at[1 - core, where],
            pair_send.at[where],
            pair_recv.at[where],
            me,
            1 - core,
        )

    loads = [
        pltpu.make_async_copy(tokens_hbm, tok.at[core, 0], local_sem.at[0]),
        pltpu.make_async_copy(gate_hbm, gate_v, local_sem.at[1]),
        pltpu.make_async_copy(up_hbm, up_v, local_sem.at[2]),
        pltpu.make_async_copy(down_hbm, down_v, local_sem.at[3]),
    ]
    start(loads)
    barrier = pltpu.get_barrier_semaphore()
    partners = [(peer_z(d), core) for d in range(1, layers)]
    partners += [(peer_a(d), core) for d in range(1, side)]
    partners += [(peer_b(d), core) for d in range(1, side)]
    partners += [(me, 1 - core)]
    for partner in partners:
        pl.semaphore_signal(barrier, inc=1, device_id=partner, device_id_type=MESH)
    named = lax.broadcasted_iota(jnp.int32, (table.shape[1], rows), 0)
    shares = jnp.zeros((table.shape[1], rows), jnp.float32)
    for k in range(routes_ref.shape[0]):
        shares += jnp.where(routes_ref[k : k + 1, :] == named, mixing_ref[k : k + 1, :], 0.0)
    table[0, :, 0:rows] = shares
    loads[0].wait()
    pl.semaphore_wait(barrier, len(partners))

    orders = [
        sorted(range(1, layers), key=lambda d: (d if d <= place else layers - d, d))
        for place in range(layers)
    ]

    def coming(k):
        return sum(jnp.where(z == place, orders[place][k], 0) for place in range(layers))

    def chain(s, way, here):
        source = slot(s, 0, 0)
        there = slot(here, 0, 0)
        to = me + (groups if way == 0 else -groups)
        return (
            remote(
                table.at[source],
                table.at[there],
                chain_send.at[2 + way, s],
                tab_recv.at[here],
                to,
            ),
            remote(
                tok.at[core, source],
                tok.at[core, there],
                chain_send.at[way, s],
                tok_recv.at[here],
                to,
            ),
        )

    def along(s, act):
        @pl.when((z < layers - 1) & (s <= z))
        def _():
            for copy in chain(s, 0, s + 1):
                act(copy)

        @pl.when((z > 0) & ((s == 0) | (s > z)))
        def _():
            for copy in chain(s, 1, (s + layers - 1) % layers):
                act(copy)

    def spread(dz):
        along(dz, lambda copy: copy.start())
        for d in range(1, side):
            start(forward(dz, d, 0))
            start(forward(dz, 0, d))
        across(slot(dz, 0, 0)).start()

    def turn(dz):
        for da in range(1, side):
            arrive(forward(dz, da, 0))
            for db in range(1, side):
                start(forward(dz, da, db))
            across(slot(dz, da, 0)).start()

    def straight(dz):
        for db in range(1, side):
            arrive(forward(dz, 0, db))
            across(slot(dz, 0, db)).start()

    def last(dz):
        for da in range(1, side):
            for db in range(1, side):
                arrive(forward(dz, da, db))
                across(slot(dz, da, db)).start()

    sequence = [0] + [coming(k) for k in range(layers - 1)]
    spread(sequence[0])
    for k in range(1, layers):
        arrive(forward(sequence[k], 0, 0))
        spread(sequence[k])
        turn(sequence[k - 1])
        straight(sequence[k - 1])
    turn(sequence[-1])

    tall = layers * rows
    tile = min(256, half)
    diagonal = lax.broadcasted_iota(jnp.int32, (rows, rows), 0) == lax.broadcasted_iota(
        jnp.int32, (rows, rows), 1
    )

    def up_project(g):
        first = g * layers
        span = pl.ds(first, layers)
        for i in range(layers):
            from_pair(first + i).wait_recv()
            mine = table[first + i, pl.ds(me, 1), 0:rows]
            column = jnp.sum(jnp.where(diagonal, mine, 0.0), axis=1, keepdims=True)
            weight[first + i] = jnp.broadcast_to(column, weight.shape[1:])

        @pl.loop(0, half // tile)
        def _(j):
            cols = pl.ds(pl.multiple_of(j * tile, tile), tile)
            left = tok[0, span].reshape(tall, width)
            right = tok[1, span].reshape(tall, width)
            gate = jnp.dot(left, gate_v[0, :, cols], preferred_element_type=jnp.float32)
            gate += jnp.dot(right, gate_v[1, :, cols], preferred_element_type=jnp.float32)
            upper = jnp.dot(left, up_v[0, :, cols], preferred_element_type=jnp.float32)
            upper += jnp.dot(right, up_v[1, :, cols], preferred_element_type=jnp.float32)
            chosen = weight[span].reshape(tall, weight.shape[2])[:, 0:1] > 0
            value = gate / (1.0 + jnp.exp(-gate)) * upper
            value = jnp.where(chosen, value, 0.0).astype(jnp.bfloat16)
            hid[core, span, :, cols] = value.reshape(layers, rows, tile)

        hidden_copy(g).start()

    def hidden_copy(g):
        span = pl.ds(g * layers, layers)
        return remote(
            hid.at[core, span],
            hid.at[core, span],
            hid_send.at[g],
            hid_recv.at[g],
            me,
            1 - core,
        )

    def hidden_from_pair(g):
        span = pl.ds(g * layers, layers)
        return remote(
            hid.at[1 - core, span],
            hid.at[1 - core, span],
            hid_send.at[g],
            hid_recv.at[g],
            me,
            1 - core,
        )

    def down_project(g):
        span = pl.ds(g * layers, layers)
        hidden_from_pair(g).wait_recv()

        @pl.loop(0, width // tile)
        def _(j):
            cols = pl.ds(pl.multiple_of(j * tile, tile), tile)
            left = hid[0, span].reshape(tall, half)
            right = hid[1, span].reshape(tall, half)
            out = jnp.dot(left, down_v[0, :, cols], preferred_element_type=jnp.float32)
            out += jnp.dot(right, down_v[1, :, cols], preferred_element_type=jnp.float32)
            out *= weight[span].reshape(tall, weight.shape[2])[:, 0:1]
            part[span, :, cols] = out.astype(jnp.bfloat16).reshape(layers, rows, tile)

    def back(dz, da, db):
        name = label(dz, da, db)
        source = part.at[slot(dz, da, db)]
        if db:
            target, to = in_b.at[db - 1, da * layers + dz], peer_b(side - db)
        elif da:
            target, to = in_a.at[da - 1, dz], peer_a(side - da)
        else:
            target, to = in_z.at[dz - 1], peer_z(layers - dz)
        return remote(source, target, back_send.at[name], back_recv.at[name], to)

    def summed(dz, da):
        total = part[slot(dz, da, 0)].astype(jnp.float32)
        for db in range(1, side):
            back(dz, da, db).wait_recv()
            total += in_b[db - 1, da * layers + dz].astype(jnp.float32)
        if da == 0:
            for d in range(1, side):
                back(dz, d, 0).wait_recv()
                total += in_a[d - 1, dz].astype(jnp.float32)
        return total

    def send_back(da, db):
        for dz in range(layers):
            back(dz, da, db).start()

    for load in loads[1:]:
        load.wait()
    up_project(0)
    straight(sequence[-1])
    edge = [g for g in range(1, groups) if g // side == 0 or g % side == 0]
    for g in edge[:-1]:
        up_project(g)
    for k in range(layers // 2):
        last(sequence[k])
    up_project(edge[-1])
    for k in range(layers // 2, layers):
        last(sequence[k])
    for db in range(1, side):
        down_project(db * stride_b)
        send_back(0, db)
    inner = [g for g in range(1, groups) if g not in edge]
    for g in inner:
        up_project(g)
    for da in range(1, side):
        down_project(da * stride_a)
    for da in range(1, side):
        for db in range(1, side):
            down_project(da * stride_a + db * stride_b)
            send_back(da, db)
    down_project(0)

    named_rows = jnp.zeros((rows, weight.shape[2]), jnp.float32)
    for s in range(weight.shape[0]):
        named_rows += (weight[s] > 0).astype(jnp.float32)
    count = jnp.sum(named_rows, axis=0, keepdims=True)[:, 0:1]
    scale = 2.0 / count
    every = weight.shape[0] * rows
    for h in range(2):

        @pl.loop(0, half // tile)
        def _(j):
            cols = pl.ds(pl.multiple_of(j * tile, tile), tile)
            gram = lax.dot_general(
                hid[core, :, :, cols].reshape(every, tile),
                hid[h].reshape(every, half),
                (((0,), (0,)), ((), ())),
                preferred_element_type=jnp.float32,
            )
            hess_v[cols, pl.ds(h * half, half)] = gram * scale

    store = pltpu.make_async_copy(hess_v, hess_hbm, local_sem.at[0])
    store.start()

    far = sorted(range(1, layers), key=lambda d: -min(d, layers - d))
    for da in range(1, side):
        for dz in far + [0]:
            part[slot(dz, da, 0)] = summed(dz, da).astype(jnp.bfloat16)
            back(dz, da, 0).start()
    for dz in far:
        part[dz] = summed(dz, 0).astype(jnp.bfloat16)
        back(dz, 0, 0).start()
    total = summed(0, 0)
    for dz in range(1, layers):
        back(dz, 0, 0).wait_recv()
        total += in_z[dz - 1].astype(jnp.float32)
    mixed_ref[...] = total.astype(jnp.bfloat16)

    store.wait()
    for da in range(side):
        for db in range(side):
            for dz in range(layers):
                across(slot(dz, da, db)).wait_send()
                if da or db:
                    for copy in forward(dz, da, db):
                        copy.wait_send()
                if dz or da or db:
                    back(dz, da, db).wait_send()
    for dz in range(layers):
        along(dz, lambda copy: copy.wait_send())
    for g in range(groups):
        hidden_copy(g).wait_send()


def settle(mixed_in, hess_in, mixed_out, hess_out, sems):
    quarter = hess_in.shape[0] // 4
    copies = [pltpu.make_async_copy(mixed_in, mixed_out, sems.at[4])]
    for i in range(4):
        span = pl.ds(i * quarter, quarter)
        copies.append(pltpu.make_async_copy(hess_in.at[span], hess_out.at[span], sems.at[i]))
    for copy in copies:
        copy.start()
    for copy in copies:
        copy.wait()


def gathered(tokens, routes, mixing, gate_weight, up_weight, down_weight):
    count = lax.axis_size("expert")
    side = math.isqrt(count // 4)
    layers = count // (side * side)
    rows, width = tokens.shape
    depth, half = gate_weight.shape[1:]
    lanes = -(-rows // 128) * 128
    bf16, f32 = jnp.bfloat16, jnp.float32
    dma = pltpu.SemaphoreType.DMA
    hbm = pl.BlockSpec(memory_space=pl.ANY)
    vmem = pl.BlockSpec(memory_space=pltpu.VMEM)
    flops = 2 * count * rows * (2 * depth * half + 2 * half * width + 2 * half * half)
    mixed, hessian = pl.pallas_call(
        functools.partial(exchange, side, layers),
        out_shape=(
            jax.ShapeDtypeStruct((rows, width), bf16),
            jax.ShapeDtypeStruct((half, 2 * half), f32),
        ),
        in_specs=[hbm, vmem, vmem, hbm, hbm, hbm],
        out_specs=(vmem, hbm),
        scratch_shapes=[
            pltpu.VMEM((2, count, rows, width), bf16),
            pltpu.VMEM((count, count, lanes), f32),
            pltpu.VMEM((count, rows, 128), f32),
            pltpu.VMEM((2, width, half), bf16),
            pltpu.VMEM((2, width, half), bf16),
            pltpu.VMEM((2, half, width), bf16),
            pltpu.VMEM((2, count, rows, half), bf16),
            pltpu.VMEM((count, rows, width), bf16),
            pltpu.VMEM((side - 1, side * layers, rows, width), bf16),
            pltpu.VMEM((side - 1, layers, rows, width), bf16),
            pltpu.VMEM((layers - 1, rows, width), bf16),
            pltpu.VMEM((half, 2 * half), f32),
            dma((4,)),
            dma((count,)),
            dma((count,)),
            dma((count,)),
            dma((count,)),
            dma((count,)),
            dma((count,)),
            dma((side * side,)),
            dma((side * side,)),
            dma((count,)),
            dma((count,)),
            dma((4, layers)),
        ],
        compiler_params=pltpu.CompilerParams(
            collective_id=0, has_side_effects=True, vmem_limit_bytes=60 * 2**20
        ),
        cost_estimate=pl.CostEstimate(
            flops=flops,
            bytes_accessed=2 * (2 * depth * half + 2 * half * width),
            transcendentals=count * rows * half,
        ),
    )(
        tokens,
        routes.T,
        mixing.T,
        gate_weight.reshape(2, width, half),
        up_weight.reshape(2, width, half),
        down_weight.reshape(2, half, width),
    )
    mixed, hessian = pl.pallas_call(
        settle,
        out_shape=(
            jax.ShapeDtypeStruct(mixed.shape, bf16),
            jax.ShapeDtypeStruct(hessian.shape, f32),
        ),
        in_specs=[hbm, hbm],
        out_specs=(hbm, hbm),
        scratch_shapes=[dma((5,))],
        compiler_params=pltpu.CompilerParams(vmem_limit_bytes=60 * 2**20),
    )(mixed, hessian)
    return (mixed, hessian[None])


def shards(tokens, routes, mixing, gate_weight, up_weight, down_weight):
    expert_count = lax.axis_size("expert")
    if 2 * routes.shape[1] >= expert_count:
        return gathered(tokens, routes, mixing, gate_weight, up_weight, down_weight)
    return dispatch(tokens, routes, mixing, gate_weight, up_weight, down_weight)


def solution(mesh):
    placed = (
        P("expert", "token"),
        P("expert", None),
        P("expert", None),
        P("expert", None, "token"),
        P("expert", None, "token"),
        P("expert", None, "token"),
    )
    return jax.shard_map(
        shards,
        mesh=mesh,
        in_specs=placed,
        out_specs=(P("expert", "token"), P("expert", "token", None)),
        check_vma=False,
    )
```

```python
import functools
import math

import jax
import jax.numpy as jnp
from jax import lax
from jax.experimental import pallas as pl
from jax.experimental.pallas import tpu as pltpu
from jax.sharding import PartitionSpec as P

MESH = pl.DeviceIdType.MESH


def dispatch(tokens, routes, mixing, gate_weight, up_weight, down_weight):
    tok_rows = tokens.shape[0]
    feat_width = tokens.shape[1]
    top_count = routes.shape[1]
    expert_count = lax.axis_size("expert")
    capacity = 2 * tok_rows * top_count // expert_count
    slot_total = expert_count * capacity
    flat_ids = routes.reshape(-1)
    chosen = (flat_ids[:, None] == jnp.arange(expert_count, dtype=jnp.int32)[None, :]).astype(
        jnp.int32
    )
    ranks = jnp.cumsum(chosen, axis=0) - chosen
    slots = jnp.sum(ranks * chosen, axis=1)
    counts = jnp.sum(chosen, axis=0)
    target = flat_ids * capacity + slots
    placing = (target[:, None] == jnp.arange(slot_total, dtype=jnp.int32)[None, :]).astype(
        jnp.bfloat16
    )
    placing = jnp.sum(placing.reshape(tok_rows, top_count, slot_total), axis=1)
    outgoing = lax.dot_general(
        placing, tokens, (((0,), (0,)), ((), ())), preferred_element_type=jnp.float32
    )
    outgoing = outgoing.astype(jnp.bfloat16).reshape(expert_count, capacity, feat_width)
    received, got_counts = (
        lax.all_to_all(outgoing, "expert", split_axis=0, concat_axis=0, tiled=True),
        lax.all_to_all(
            counts.astype(jnp.bfloat16), "expert", split_axis=0, concat_axis=0, tiled=True
        ),
    )
    rows_in = received.reshape(slot_total, feat_width)
    row_total = jnp.sum(got_counts.astype(jnp.float32))
    gate_local = gate_weight[0]
    up_local = up_weight[0]
    piece = lax.all_gather(rows_in, "token", axis=1, tiled=True)
    gate = jnp.dot(piece, gate_local, preferred_element_type=jnp.float32)
    upper = jnp.dot(piece, up_local, preferred_element_type=jnp.float32)
    hidden = (jax.nn.silu(gate) * upper).astype(jnp.bfloat16)
    down_local = down_weight[0]
    piece = lax.all_gather(hidden, "token", axis=1, tiled=True)
    out_sum = jnp.dot(piece, down_local, preferred_element_type=jnp.float32)
    outer = lax.dot_general(
        hidden, piece, (((0,), (0,)), ((), ())), preferred_element_type=jnp.float32
    )
    gram = outer
    out_sum, gram = (out_sum, gram)
    hessian = (2.0 / row_total * gram)[None]
    expert_out = out_sum.astype(jnp.bfloat16).reshape(expert_count, capacity, feat_width)
    returned = lax.all_to_all(expert_out, "expert", split_axis=0, concat_axis=0, tiled=True)
    picked = returned.reshape(slot_total, feat_width)[target]
    picked = picked.reshape(tok_rows, top_count, feat_width).astype(jnp.float32)
    mixed = jnp.sum(picked * mixing[:, :, None], axis=1).astype(jnp.bfloat16)
    return (mixed, hessian)


def exchange(
    side,
    layers,
    tokens_hbm,
    routes_ref,
    mixing_ref,
    gate_hbm,
    up_hbm,
    down_hbm,
    mixed_ref,
    hess_hbm,
    tok,
    table,
    weight,
    gate_v,
    up_v,
    down_v,
    hid,
    part,
    in_b,
    in_a,
    in_z,
    hess_v,
    local_sem,
    tok_send,
    tok_recv,
    tab_send,
    tab_recv,
    pair_send,
    pair_recv,
    hid_send,
    hid_recv,
    back_send,
    back_recv,
    chain_send,
):
    groups = side * side
    rows, width = mixed_ref.shape
    half = gate_v.shape[2]
    me = lax.axis_index("expert")
    core = lax.axis_index("token")
    z, y, x = me // groups, (me // side) % side, me % side
    stride_a = jnp.where(core == 0, side, 1)
    stride_b = jnp.where(core == 0, 1, side)
    pos_a = jnp.where(core == 0, y, x)
    pos_b = jnp.where(core == 0, x, y)

    def peer_z(step):
        return me + ((z + step) % layers - z) * groups

    def peer_a(step):
        return me + ((pos_a + step) % side - pos_a) * stride_a

    def peer_b(step):
        return me + ((pos_b + step) % side - pos_b) * stride_b

    def slot(dz, da, db):
        return (da * stride_a + db * stride_b) * layers + dz

    def label(dz, da, db):
        return (da * side + db) * layers + dz

    def remote(src, dst, send, recv, to, to_core=None):
        return pltpu.make_async_remote_copy(
            src_ref=src,
            dst_ref=dst,
            send_sem=send,
            recv_sem=recv,
            device_id=(to, core if to_core is None else to_core),
            device_id_type=MESH,
        )

    def forward(dz, da, db):
        if db:
            source, to = slot(dz, da, 0), peer_b(db)
        elif da:
            source, to = slot(dz, 0, 0), peer_a(da)
        else:
            source, to = slot(0, 0, 0), peer_z(dz)
        name = label(dz, da, db)
        here = slot(dz, da, db)
        return (
            remote(table.at[source], table.at[here], tab_send.at[name], tab_recv.at[name], to),
            remote(
                tok.at[core, source],
                tok.at[core, here],
                tok_send.at[name],
                tok_recv.at[name],
                to,
            ),
        )

    def start(copies):
        for copy in copies:
            copy.start()

    def arrive(copies):
        for copy in copies:
            copy.wait_recv()

    def across(where):
        return remote(
            tok.at[core, where],
            tok.at[core, where],
            pair_send.at[where],
            pair_recv.at[where],
            me,
            1 - core,
        )

    def from_pair(where):
        return remote(
            tok.at[1 - core, where],
            tok.at[1 - core, where],
            pair_send.at[where],
            pair_recv.at[where],
            me,
            1 - core,
        )

    loads = [
        pltpu.make_async_copy(tokens_hbm, tok.at[core, 0], local_sem.at[0]),
        pltpu.make_async_copy(gate_hbm, gate_v, local_sem.at[1]),
        pltpu.make_async_copy(up_hbm, up_v, local_sem.at[2]),
        pltpu.make_async_copy(down_hbm, down_v, local_sem.at[3]),
    ]
    start(loads)
    barrier = pltpu.get_barrier_semaphore()
    partners = [(peer_z(d), core) for d in range(1, layers)]
    partners += [(peer_a(d), core) for d in range(1, side)]
    partners += [(peer_b(d), core) for d in range(1, side)]
    partners += [(me, 1 - core)]
    for partner in partners:
        pl.semaphore_signal(barrier, inc=1, device_id=partner, device_id_type=MESH)
    named = lax.broadcasted_iota(jnp.int32, (table.shape[1], rows), 0)
    shares = jnp.zeros((table.shape[1], rows), jnp.float32)
    for k in range(routes_ref.shape[0]):
        shares += jnp.where(routes_ref[k : k + 1, :] == named, mixing_ref[k : k + 1, :], 0.0)
    table[0, :, 0:rows] = shares
    loads[0].wait()
    pl.semaphore_wait(barrier, len(partners))

    orders = [
        sorted(range(1, layers), key=lambda d: (d if d <= place else layers - d, d))
        for place in range(layers)
    ]

    def coming(k):
        return sum(jnp.where(z == place, orders[place][k], 0) for place in range(layers))

    def chain(s, way, here):
        source = slot(s, 0, 0)
        there = slot(here, 0, 0)
        to = me + (groups if way == 0 else -groups)
        return (
            remote(
                table.at[source],
                table.at[there],
                chain_send.at[2 + way, s],
                tab_recv.at[here],
                to,
            ),
            remote(
                tok.at[core, source],
                tok.at[core, there],
                chain_send.at[way, s],
                tok_recv.at[here],
                to,
            ),
        )

    def along(s, act):
        @pl.when((z < layers - 1) & (s <= z))
        def _():
            for copy in chain(s, 0, s + 1):
                act(copy)

        @pl.when((z > 0) & ((s == 0) | (s > z)))
        def _():
            for copy in chain(s, 1, (s + layers - 1) % layers):
                act(copy)

    def spread(dz):
        along(dz, lambda copy: copy.start())
        for d in range(1, side):
            start(forward(dz, d, 0))
            start(forward(dz, 0, d))
        across(slot(dz, 0, 0)).start()

    def turn(dz):
        for da in range(1, side):
            arrive(forward(dz, da, 0))
            across(slot(dz, da, 0)).start()

    def finish(dz):
        for da in range(1, side):
            for db in range(1, side):
                start(forward(dz, da, db))

    def straight(dz):
        for db in range(1, side):
            arrive(forward(dz, 0, db))
            across(slot(dz, 0, db)).start()

    def last(dz):
        for da in range(1, side):
            for db in range(1, side):
                arrive(forward(dz, da, db))
                across(slot(dz, da, db)).start()

    sequence = [0] + [coming(k) for k in range(layers - 1)]
    spread(sequence[0])
    for k in range(1, layers):
        arrive(forward(sequence[k], 0, 0))
        spread(sequence[k])
        turn(sequence[k - 1])
        straight(sequence[k - 1])
    for k in range(layers - 1):
        finish(sequence[k])
    turn(sequence[-1])
    finish(sequence[-1])

    tall = layers * rows
    tile = min(256, half)
    diagonal = lax.broadcasted_iota(jnp.int32, (rows, rows), 0) == lax.broadcasted_iota(
        jnp.int32, (rows, rows), 1
    )

    def up_project(g):
        first = g * layers
        span = pl.ds(first, layers)
        for i in range(layers):
            from_pair(first + i).wait_recv()
            mine = table[first + i, pl.ds(me, 1), 0:rows]
            column = jnp.sum(jnp.where(diagonal, mine, 0.0), axis=1, keepdims=True)
            weight[first + i] = jnp.broadcast_to(column, weight.shape[1:])

        @pl.loop(0, half // tile)
        def _(j):
            cols = pl.ds(pl.multiple_of(j * tile, tile), tile)
            left = tok[0, span].reshape(tall, width)
            right = tok[1, span].reshape(tall, width)
            gate = jnp.dot(left, gate_v[0, :, cols], preferred_element_type=jnp.float32)
            gate += jnp.dot(right, gate_v[1, :, cols], preferred_element_type=jnp.float32)
            upper = jnp.dot(left, up_v[0, :, cols], preferred_element_type=jnp.float32)
            upper += jnp.dot(right, up_v[1, :, cols], preferred_element_type=jnp.float32)
            chosen = weight[span].reshape(tall, weight.shape[2])[:, 0:1] > 0
            value = gate / (1.0 + jnp.exp(-gate)) * upper
            value = jnp.where(chosen, value, 0.0).astype(jnp.bfloat16)
            hid[core, span, :, cols] = value.reshape(layers, rows, tile)

        hidden_copy(g).start()

    def hidden_copy(g):
        span = pl.ds(g * layers, layers)
        return remote(
            hid.at[core, span],
            hid.at[core, span],
            hid_send.at[g],
            hid_recv.at[g],
            me,
            1 - core,
        )

    def hidden_from_pair(g):
        span = pl.ds(g * layers, layers)
        return remote(
            hid.at[1 - core, span],
            hid.at[1 - core, span],
            hid_send.at[g],
            hid_recv.at[g],
            me,
            1 - core,
        )

    def down_project(g):
        span = pl.ds(g * layers, layers)
        hidden_from_pair(g).wait_recv()

        @pl.loop(0, width // tile)
        def _(j):
            cols = pl.ds(pl.multiple_of(j * tile, tile), tile)
            left = hid[0, span].reshape(tall, half)
            right = hid[1, span].reshape(tall, half)
            out = jnp.dot(left, down_v[0, :, cols], preferred_element_type=jnp.float32)
            out += jnp.dot(right, down_v[1, :, cols], preferred_element_type=jnp.float32)
            out *= weight[span].reshape(tall, weight.shape[2])[:, 0:1]
            part[span, :, cols] = out.astype(jnp.bfloat16).reshape(layers, rows, tile)

    def back(dz, da, db):
        name = label(dz, da, db)
        source = part.at[slot(dz, da, db)]
        if db:
            target, to = in_b.at[db - 1, da * layers + dz], peer_b(side - db)
        elif da:
            target, to = in_a.at[da - 1, dz], peer_a(side - da)
        else:
            target, to = in_z.at[dz - 1], peer_z(layers - dz)
        return remote(source, target, back_send.at[name], back_recv.at[name], to)

    def summed(dz, da):
        total = part[slot(dz, da, 0)].astype(jnp.float32)
        for db in range(1, side):
            back(dz, da, db).wait_recv()
            total += in_b[db - 1, da * layers + dz].astype(jnp.float32)
        if da == 0:
            for d in range(1, side):
                back(dz, d, 0).wait_recv()
                total += in_a[d - 1, dz].astype(jnp.float32)
        return total

    far = sorted(range(1, layers), key=lambda d: -min(d, layers - d))

    def send_back(da, db):
        for dz in far + [0]:
            back(dz, da, db).start()

    for load in loads[1:]:
        load.wait()
    up_project(0)
    straight(sequence[-1])
    edge = [g for g in range(1, groups) if g // side == 0 or g % side == 0]
    for g in edge[:-1]:
        up_project(g)
    for k in range(layers // 2):
        last(sequence[k])
    up_project(edge[-1])
    for k in range(layers // 2, layers):
        last(sequence[k])
    for db in range(1, side):
        down_project(db * stride_b)
        send_back(0, db)
    inner = [g for g in range(1, groups) if g not in edge]
    for g in inner:
        up_project(g)
    for da in range(1, side):
        down_project(da * stride_a)
    for da in range(1, side):
        for db in range(1, side):
            down_project(da * stride_a + db * stride_b)
            send_back(da, db)
    down_project(0)

    named_rows = jnp.zeros((rows, weight.shape[2]), jnp.float32)
    for s in range(weight.shape[0]):
        named_rows += (weight[s] > 0).astype(jnp.float32)
    count = jnp.sum(named_rows, axis=0, keepdims=True)[:, 0:1]
    scale = 2.0 / count
    every = weight.shape[0] * rows

    def hessian_half(h):
        @pl.loop(0, half // tile)
        def _(j):
            cols = pl.ds(pl.multiple_of(j * tile, tile), tile)
            gram = lax.dot_general(
                hid[core, :, :, cols].reshape(every, tile),
                hid[h].reshape(every, half),
                (((0,), (0,)), ((), ())),
                preferred_element_type=jnp.float32,
            )
            hess_v[cols, pl.ds(h * half, half)] = gram * scale

    hessian_half(0)
    for da in range(1, side):
        for dz in far + [0]:
            part[slot(dz, da, 0)] = summed(dz, da).astype(jnp.bfloat16)
            back(dz, da, 0).start()
    hessian_half(1)
    store = pltpu.make_async_copy(hess_v, hess_hbm, local_sem.at[0])
    store.start()
    for dz in far:
        part[dz] = summed(dz, 0).astype(jnp.bfloat16)
        back(dz, 0, 0).start()
    total = summed(0, 0)
    for dz in range(1, layers):
        back(dz, 0, 0).wait_recv()
        total += in_z[dz - 1].astype(jnp.float32)
    mixed_ref[...] = total.astype(jnp.bfloat16)

    store.wait()
    for da in range(side):
        for db in range(side):
            for dz in range(layers):
                across(slot(dz, da, db)).wait_send()
                if da or db:
                    for copy in forward(dz, da, db):
                        copy.wait_send()
                if dz or da or db:
                    back(dz, da, db).wait_send()
    for dz in range(layers):
        along(dz, lambda copy: copy.wait_send())
    for g in range(groups):
        hidden_copy(g).wait_send()


def settle(mixed_in, hess_in, mixed_out, hess_out, mixed_v, hess_v, sems):
    pieces = 4
    span = hess_in.shape[0] // pieces
    moves = [(mixed_in, mixed_v, mixed_out)]
    for i in range(pieces):
        moves.append([ref.at[pl.ds(i * span, span)] for ref in (hess_in, hess_v, hess_out)])
    comes = [pltpu.make_async_copy(m[0], m[1], sems.at[0, i]) for i, m in enumerate(moves)]
    goes = [pltpu.make_async_copy(m[1], m[2], sems.at[1, i]) for i, m in enumerate(moves)]
    for copy in comes:
        copy.start()
    for come, go in zip(comes, goes):
        come.wait()
        go.start()
    for go in goes:
        go.wait()


def gathered(tokens, routes, mixing, gate_weight, up_weight, down_weight):
    count = lax.axis_size("expert")
    side = math.isqrt(count // 4)
    layers = count // (side * side)
    rows, width = tokens.shape
    depth, half = gate_weight.shape[1:]
    lanes = -(-rows // 128) * 128
    bf16, f32 = jnp.bfloat16, jnp.float32
    dma = pltpu.SemaphoreType.DMA
    hbm = pl.BlockSpec(memory_space=pl.ANY)
    vmem = pl.BlockSpec(memory_space=pltpu.VMEM)
    flops = 2 * count * rows * (2 * depth * half + 2 * half * width + 2 * half * half)
    mixed, hessian = pl.pallas_call(
        functools.partial(exchange, side, layers),
        out_shape=(
            jax.ShapeDtypeStruct((rows, width), bf16),
            jax.ShapeDtypeStruct((half, 2 * half), f32),
        ),
        in_specs=[hbm, vmem, vmem, hbm, hbm, hbm],
        out_specs=(vmem, hbm),
        scratch_shapes=[
            pltpu.VMEM((2, count, rows, width), bf16),
            pltpu.VMEM((count, count, lanes), f32),
            pltpu.VMEM((count, rows, 128), f32),
            pltpu.VMEM((2, width, half), bf16),
            pltpu.VMEM((2, width, half), bf16),
            pltpu.VMEM((2, half, width), bf16),
            pltpu.VMEM((2, count, rows, half), bf16),
            pltpu.VMEM((count, rows, width), bf16),
            pltpu.VMEM((side - 1, side * layers, rows, width), bf16),
            pltpu.VMEM((side - 1, layers, rows, width), bf16),
            pltpu.VMEM((layers - 1, rows, width), bf16),
            pltpu.VMEM((half, 2 * half), f32),
            dma((4,)),
            dma((count,)),
            dma((count,)),
            dma((count,)),
            dma((count,)),
            dma((count,)),
            dma((count,)),
            dma((side * side,)),
            dma((side * side,)),
            dma((count,)),
            dma((count,)),
            dma((4, layers)),
        ],
        compiler_params=pltpu.CompilerParams(
            collective_id=0, has_side_effects=True, vmem_limit_bytes=60 * 2**20
        ),
        cost_estimate=pl.CostEstimate(
            flops=flops,
            bytes_accessed=2 * (2 * depth * half + 2 * half * width),
            transcendentals=count * rows * half,
        ),
    )(
        tokens,
        routes.T,
        mixing.T,
        gate_weight.reshape(2, width, half),
        up_weight.reshape(2, width, half),
        down_weight.reshape(2, half, width),
    )
    mixed, hessian = pl.pallas_call(
        settle,
        out_shape=(
            jax.ShapeDtypeStruct(mixed.shape, bf16),
            jax.ShapeDtypeStruct(hessian.shape, f32),
        ),
        in_specs=[hbm, hbm],
        out_specs=(hbm, hbm),
        scratch_shapes=[
            pltpu.VMEM(mixed.shape, bf16),
            pltpu.VMEM(hessian.shape, f32),
            dma((2, 5)),
        ],
        compiler_params=pltpu.CompilerParams(vmem_limit_bytes=60 * 2**20),
    )(mixed, hessian)
    return (mixed, hessian[None])


def shards(tokens, routes, mixing, gate_weight, up_weight, down_weight):
    expert_count = lax.axis_size("expert")
    if 2 * routes.shape[1] >= expert_count:
        return gathered(tokens, routes, mixing, gate_weight, up_weight, down_weight)
    return dispatch(tokens, routes, mixing, gate_weight, up_weight, down_weight)


def solution(mesh):
    placed = (
        P("expert", "token"),
        P("expert", None),
        P("expert", None),
        P("expert", None, "token"),
        P("expert", None, "token"),
        P("expert", None, "token"),
    )
    return jax.shard_map(
        shards,
        mesh=mesh,
        in_specs=placed,
        out_specs=(P("expert", "token"), P("expert", "token", None)),
        check_vma=False,
    )
```

```python
import functools
import math

import jax
import jax.numpy as jnp
from jax import lax
from jax.experimental import pallas as pl
from jax.experimental.pallas import tpu as pltpu
from jax.sharding import PartitionSpec as P

MESH = pl.DeviceIdType.MESH


def dispatch(tokens, routes, mixing, gate_weight, up_weight, down_weight):
    tok_rows = tokens.shape[0]
    feat_width = tokens.shape[1]
    top_count = routes.shape[1]
    expert_count = lax.axis_size("expert")
    capacity = 2 * tok_rows * top_count // expert_count
    slot_total = expert_count * capacity
    flat_ids = routes.reshape(-1)
    chosen = (flat_ids[:, None] == jnp.arange(expert_count, dtype=jnp.int32)[None, :]).astype(
        jnp.int32
    )
    ranks = jnp.cumsum(chosen, axis=0) - chosen
    slots = jnp.sum(ranks * chosen, axis=1)
    counts = jnp.sum(chosen, axis=0)
    target = flat_ids * capacity + slots
    placing = (target[:, None] == jnp.arange(slot_total, dtype=jnp.int32)[None, :]).astype(
        jnp.bfloat16
    )
    placing = jnp.sum(placing.reshape(tok_rows, top_count, slot_total), axis=1)
    outgoing = lax.dot_general(
        placing, tokens, (((0,), (0,)), ((), ())), preferred_element_type=jnp.float32
    )
    outgoing = outgoing.astype(jnp.bfloat16).reshape(expert_count, capacity, feat_width)
    received, got_counts = (
        lax.all_to_all(outgoing, "expert", split_axis=0, concat_axis=0, tiled=True),
        lax.all_to_all(
            counts.astype(jnp.bfloat16), "expert", split_axis=0, concat_axis=0, tiled=True
        ),
    )
    rows_in = received.reshape(slot_total, feat_width)
    row_total = jnp.sum(got_counts.astype(jnp.float32))
    gate_local = gate_weight[0]
    up_local = up_weight[0]
    piece = lax.all_gather(rows_in, "token", axis=1, tiled=True)
    gate = jnp.dot(piece, gate_local, preferred_element_type=jnp.float32)
    upper = jnp.dot(piece, up_local, preferred_element_type=jnp.float32)
    hidden = (jax.nn.silu(gate) * upper).astype(jnp.bfloat16)
    down_local = down_weight[0]
    piece = lax.all_gather(hidden, "token", axis=1, tiled=True)
    out_sum = jnp.dot(piece, down_local, preferred_element_type=jnp.float32)
    outer = lax.dot_general(
        hidden, piece, (((0,), (0,)), ((), ())), preferred_element_type=jnp.float32
    )
    gram = outer
    out_sum, gram = (out_sum, gram)
    hessian = (2.0 / row_total * gram)[None]
    expert_out = out_sum.astype(jnp.bfloat16).reshape(expert_count, capacity, feat_width)
    returned = lax.all_to_all(expert_out, "expert", split_axis=0, concat_axis=0, tiled=True)
    picked = returned.reshape(slot_total, feat_width)[target]
    picked = picked.reshape(tok_rows, top_count, feat_width).astype(jnp.float32)
    mixed = jnp.sum(picked * mixing[:, :, None], axis=1).astype(jnp.bfloat16)
    return (mixed, hessian)


def exchange(
    side,
    layers,
    tokens_hbm,
    routes_ref,
    mixing_ref,
    gate_hbm,
    up_hbm,
    down_hbm,
    mixed_ref,
    hess_hbm,
    tok,
    table,
    weight,
    gate_v,
    up_v,
    down_v,
    hid,
    part,
    in_b,
    in_a,
    in_z,
    hess_v,
    local_sem,
    tok_send,
    tok_recv,
    tab_send,
    tab_recv,
    pair_send,
    pair_recv,
    hid_send,
    hid_recv,
    back_send,
    back_recv,
    chain_send,
):
    groups = side * side
    rows, width = mixed_ref.shape
    half = gate_v.shape[2]
    me = lax.axis_index("expert")
    core = lax.axis_index("token")
    z, y, x = me // groups, (me // side) % side, me % side
    stride_a = jnp.where(core == 0, side, 1)
    stride_b = jnp.where(core == 0, 1, side)
    pos_a = jnp.where(core == 0, y, x)
    pos_b = jnp.where(core == 0, x, y)

    def peer_z(step):
        return me + ((z + step) % layers - z) * groups

    def peer_a(step):
        return me + ((pos_a + step) % side - pos_a) * stride_a

    def peer_b(step):
        return me + ((pos_b + step) % side - pos_b) * stride_b

    def slot(dz, da, db):
        return (da * stride_a + db * stride_b) * layers + dz

    def label(dz, da, db):
        return (da * side + db) * layers + dz

    def remote(src, dst, send, recv, to, to_core=None):
        return pltpu.make_async_remote_copy(
            src_ref=src,
            dst_ref=dst,
            send_sem=send,
            recv_sem=recv,
            device_id=(to, core if to_core is None else to_core),
            device_id_type=MESH,
        )

    def forward(dz, da, db):
        if db:
            source, to = slot(dz, da, 0), peer_b(db)
        elif da:
            source, to = slot(dz, 0, 0), peer_a(da)
        else:
            source, to = slot(0, 0, 0), peer_z(dz)
        name = label(dz, da, db)
        here = slot(dz, da, db)
        return (
            remote(table.at[source], table.at[here], tab_send.at[name], tab_recv.at[name], to),
            remote(
                tok.at[core, source],
                tok.at[core, here],
                tok_send.at[name],
                tok_recv.at[name],
                to,
            ),
        )

    def start(copies):
        for copy in copies:
            copy.start()

    def arrive(copies):
        for copy in copies:
            copy.wait_recv()

    def across(where):
        return remote(
            tok.at[core, where],
            tok.at[core, where],
            pair_send.at[where],
            pair_recv.at[where],
            me,
            1 - core,
        )

    def from_pair(where):
        return remote(
            tok.at[1 - core, where],
            tok.at[1 - core, where],
            pair_send.at[where],
            pair_recv.at[where],
            me,
            1 - core,
        )

    loads = [
        pltpu.make_async_copy(tokens_hbm, tok.at[core, 0], local_sem.at[0]),
        pltpu.make_async_copy(gate_hbm, gate_v, local_sem.at[1]),
        pltpu.make_async_copy(up_hbm, up_v, local_sem.at[2]),
        pltpu.make_async_copy(down_hbm, down_v, local_sem.at[3]),
    ]
    start(loads)
    barrier = pltpu.get_barrier_semaphore()
    partners = [(peer_z(d), core) for d in range(1, layers)]
    partners += [(peer_a(d), core) for d in range(1, side)]
    partners += [(peer_b(d), core) for d in range(1, side)]
    partners += [(me, 1 - core)]
    for partner in partners:
        pl.semaphore_signal(barrier, inc=1, device_id=partner, device_id_type=MESH)
    named = lax.broadcasted_iota(jnp.int32, (table.shape[1], rows), 0)
    shares = jnp.zeros((table.shape[1], rows), jnp.float32)
    for k in range(routes_ref.shape[0]):
        shares += jnp.where(routes_ref[k : k + 1, :] == named, mixing_ref[k : k + 1, :], 0.0)
    table[0, :, 0:rows] = shares
    loads[0].wait()
    pl.semaphore_wait(barrier, len(partners))

    orders = [
        sorted(range(1, layers), key=lambda d: (d if d <= place else layers - d, d))
        for place in range(layers)
    ]

    def coming(k):
        return sum(jnp.where(z == place, orders[place][k], 0) for place in range(layers))

    def chain(s, way, here):
        source = slot(s, 0, 0)
        there = slot(here, 0, 0)
        to = me + (groups if way == 0 else -groups)
        return (
            remote(
                table.at[source],
                table.at[there],
                chain_send.at[2 + way, s],
                tab_recv.at[here],
                to,
            ),
            remote(
                tok.at[core, source],
                tok.at[core, there],
                chain_send.at[way, s],
                tok_recv.at[here],
                to,
            ),
        )

    def along(s, act):
        @pl.when((z < layers - 1) & (s <= z))
        def _():
            for copy in chain(s, 0, s + 1):
                act(copy)

        @pl.when((z > 0) & ((s == 0) | (s > z)))
        def _():
            for copy in chain(s, 1, (s + layers - 1) % layers):
                act(copy)

    def spread(dz):
        along(dz, lambda copy: copy.start())
        for d in range(1, side):
            start(forward(dz, d, 0))
            start(forward(dz, 0, d))
        across(slot(dz, 0, 0)).start()

    def turn(dz):
        for da in range(1, side):
            arrive(forward(dz, da, 0))
            for db in range(1, side):
                start(forward(dz, da, db))
            across(slot(dz, da, 0)).start()

    def straight(dz):
        for db in range(1, side):
            arrive(forward(dz, 0, db))
            across(slot(dz, 0, db)).start()

    def last(dz):
        for da in range(1, side):
            for db in range(1, side):
                arrive(forward(dz, da, db))
                across(slot(dz, da, db)).start()

    sequence = [0] + [coming(k) for k in range(layers - 1)]
    spread(sequence[0])
    for k in range(1, layers):
        arrive(forward(sequence[k], 0, 0))
        spread(sequence[k])
        turn(sequence[k - 1])
        straight(sequence[k - 1])
    turn(sequence[-1])

    tall = layers * rows
    tile = min(256, half)
    diagonal = lax.broadcasted_iota(jnp.int32, (rows, rows), 0) == lax.broadcasted_iota(
        jnp.int32, (rows, rows), 1
    )

    def row_weights(span, count):
        wide = weight[span].reshape(count, weight.shape[2])
        return jnp.concatenate([wide] * (tile // weight.shape[2]), axis=1)

    def up_project(g, many=1):
        first = g * layers
        blocks = many * layers
        tall = blocks * rows
        span = pl.ds(first, blocks)
        for i in range(blocks):
            from_pair(first + i).wait_recv()
            mine = table[first + i, pl.ds(me, 1), 0:rows]
            column = jnp.sum(jnp.where(diagonal, mine, 0.0), axis=1, keepdims=True)
            weight[first + i] = jnp.broadcast_to(column, weight.shape[1:])

        @pl.loop(0, half // tile)
        def _(j):
            cols = pl.ds(pl.multiple_of(j * tile, tile), tile)
            left = tok[0, span].reshape(tall, width)
            right = tok[1, span].reshape(tall, width)
            gate = jnp.dot(left, gate_v[0, :, cols], preferred_element_type=jnp.float32)
            gate += jnp.dot(right, gate_v[1, :, cols], preferred_element_type=jnp.float32)
            upper = jnp.dot(left, up_v[0, :, cols], preferred_element_type=jnp.float32)
            upper += jnp.dot(right, up_v[1, :, cols], preferred_element_type=jnp.float32)
            chosen = row_weights(span, tall) > 0
            value = gate / (1.0 + jnp.exp(-gate)) * upper
            value = jnp.where(chosen, value, 0.0).astype(jnp.bfloat16)
            hid[core, span, :, cols] = value.reshape(blocks, rows, tile)

        for each in range(g, g + many):
            hidden_copy(each).start()

    def hidden_copy(g):
        span = pl.ds(g * layers, layers)
        return remote(
            hid.at[core, span],
            hid.at[core, span],
            hid_send.at[g],
            hid_recv.at[g],
            me,
            1 - core,
        )

    def hidden_from_pair(g):
        span = pl.ds(g * layers, layers)
        return remote(
            hid.at[1 - core, span],
            hid.at[1 - core, span],
            hid_send.at[g],
            hid_recv.at[g],
            me,
            1 - core,
        )

    def down_project(g):
        span = pl.ds(g * layers, layers)
        hidden_from_pair(g).wait_recv()

        @pl.loop(0, width // tile)
        def _(j):
            cols = pl.ds(pl.multiple_of(j * tile, tile), tile)
            left = hid[0, span].reshape(tall, half)
            right = hid[1, span].reshape(tall, half)
            out = jnp.dot(left, down_v[0, :, cols], preferred_element_type=jnp.float32)
            out += jnp.dot(right, down_v[1, :, cols], preferred_element_type=jnp.float32)
            out *= row_weights(span, tall)
            part[span, :, cols] = out.astype(jnp.bfloat16).reshape(layers, rows, tile)

    def back(dz, da, db):
        name = label(dz, da, db)
        source = part.at[slot(dz, da, db)]
        if db:
            target, to = in_b.at[db - 1, da * layers + dz], peer_b(side - db)
        elif da:
            target, to = in_a.at[da - 1, dz], peer_a(side - da)
        else:
            target, to = in_z.at[dz - 1], peer_z(layers - dz)
        return remote(source, target, back_send.at[name], back_recv.at[name], to)

    def summed(dz, da):
        total = part[slot(dz, da, 0)].astype(jnp.float32)
        for db in range(1, side):
            back(dz, da, db).wait_recv()
            total += in_b[db - 1, da * layers + dz].astype(jnp.float32)
        if da == 0:
            for d in range(1, side):
                back(dz, d, 0).wait_recv()
                total += in_a[d - 1, dz].astype(jnp.float32)
        return total

    far = sorted(range(1, layers), key=lambda d: -min(d, layers - d))

    def send_back(da, db):
        for dz in far + [0]:
            back(dz, da, db).start()

    for load in loads[1:]:
        load.wait()
    up_project(0)
    straight(sequence[-1])
    edge = [g for g in range(1, groups) if g // side == 0 or g % side == 0]
    inner = [g for g in range(1, groups) if g not in edge]
    if edge == list(range(edge[0], edge[-1] + 1)):
        up_project(edge[0], len(edge))
    else:
        for g in edge:
            up_project(g)
    for k in range(layers):
        last(sequence[k])
    for db in range(1, side):
        down_project(db * stride_b)
        send_back(0, db)
    for g in inner:
        up_project(g)
    for da in range(1, side):
        down_project(da * stride_a)
    for da in range(1, side):
        for db in range(1, side):
            down_project(da * stride_a + db * stride_b)
            send_back(da, db)
    down_project(0)

    named_rows = jnp.zeros((rows, weight.shape[2]), jnp.float32)
    for s in range(weight.shape[0]):
        named_rows += (weight[s] > 0).astype(jnp.float32)
    count = jnp.sum(named_rows, axis=0, keepdims=True)[:, 0:1]
    scale = 2.0 / count
    every = weight.shape[0] * rows

    def hessian_half(h):
        @pl.loop(0, half // tile)
        def _(j):
            cols = pl.ds(pl.multiple_of(j * tile, tile), tile)
            gram = lax.dot_general(
                hid[core, :, :, cols].reshape(every, tile),
                hid[h].reshape(every, half),
                (((0,), (0,)), ((), ())),
                preferred_element_type=jnp.float32,
            )
            hess_v[cols, pl.ds(h * half, half)] = gram * scale

    hessian_half(0)
    for da in range(1, side):
        for dz in far + [0]:
            part[slot(dz, da, 0)] = summed(dz, da).astype(jnp.bfloat16)
            back(dz, da, 0).start()
    hessian_half(1)
    store = pltpu.make_async_copy(hess_v, hess_hbm, local_sem.at[0])
    store.start()
    for dz in far:
        part[dz] = summed(dz, 0).astype(jnp.bfloat16)
        back(dz, 0, 0).start()
    total = summed(0, 0)
    for dz in range(1, layers):
        back(dz, 0, 0).wait_recv()
        total += in_z[dz - 1].astype(jnp.float32)
    mixed_ref[...] = total.astype(jnp.bfloat16)

    store.wait()
    for da in range(side):
        for db in range(side):
            for dz in range(layers):
                across(slot(dz, da, db)).wait_send()
                if da or db:
                    for copy in forward(dz, da, db):
                        copy.wait_send()
                if dz or da or db:
                    back(dz, da, db).wait_send()
    for dz in range(layers):
        along(dz, lambda copy: copy.wait_send())
    for g in range(groups):
        hidden_copy(g).wait_send()


def settle(mixed_in, hess_in, mixed_out, hess_out, mixed_v, hess_v, sems):
    pieces = 4
    span = hess_in.shape[0] // pieces
    moves = [(mixed_in, mixed_v, mixed_out)]
    for i in range(pieces):
        moves.append([ref.at[pl.ds(i * span, span)] for ref in (hess_in, hess_v, hess_out)])
    comes = [pltpu.make_async_copy(m[0], m[1], sems.at[0, i]) for i, m in enumerate(moves)]
    goes = [pltpu.make_async_copy(m[1], m[2], sems.at[1, i]) for i, m in enumerate(moves)]
    for copy in comes:
        copy.start()
    for come, go in zip(comes, goes):
        come.wait()
        go.start()
    for go in goes:
        go.wait()


def gathered(tokens, routes, mixing, gate_weight, up_weight, down_weight):
    count = lax.axis_size("expert")
    side = math.isqrt(count // 4)
    layers = count // (side * side)
    rows, width = tokens.shape
    depth, half = gate_weight.shape[1:]
    lanes = -(-rows // 128) * 128
    bf16, f32 = jnp.bfloat16, jnp.float32
    dma = pltpu.SemaphoreType.DMA
    hbm = pl.BlockSpec(memory_space=pl.ANY)
    vmem = pl.BlockSpec(memory_space=pltpu.VMEM)
    flops = 2 * count * rows * (2 * depth * half + 2 * half * width + 2 * half * half)
    mixed, hessian = pl.pallas_call(
        functools.partial(exchange, side, layers),
        out_shape=(
            jax.ShapeDtypeStruct((rows, width), bf16),
            jax.ShapeDtypeStruct((half, 2 * half), f32),
        ),
        in_specs=[hbm, vmem, vmem, hbm, hbm, hbm],
        out_specs=(vmem, hbm),
        scratch_shapes=[
            pltpu.VMEM((2, count, rows, width), bf16),
            pltpu.VMEM((count, count, lanes), f32),
            pltpu.VMEM((count, rows, 128), f32),
            pltpu.VMEM((2, width, half), bf16),
            pltpu.VMEM((2, width, half), bf16),
            pltpu.VMEM((2, half, width), bf16),
            pltpu.VMEM((2, count, rows, half), bf16),
            pltpu.VMEM((count, rows, width), bf16),
            pltpu.VMEM((side - 1, side * layers, rows, width), bf16),
            pltpu.VMEM((side - 1, layers, rows, width), bf16),
            pltpu.VMEM((layers - 1, rows, width), bf16),
            pltpu.VMEM((half, 2 * half), f32),
            dma((4,)),
            dma((count,)),
            dma((count,)),
            dma((count,)),
            dma((count,)),
            dma((count,)),
            dma((count,)),
            dma((side * side,)),
            dma((side * side,)),
            dma((count,)),
            dma((count,)),
            dma((4, layers)),
        ],
        compiler_params=pltpu.CompilerParams(
            collective_id=0, has_side_effects=True, vmem_limit_bytes=60 * 2**20
        ),
        cost_estimate=pl.CostEstimate(
            flops=flops,
            bytes_accessed=2 * (2 * depth * half + 2 * half * width),
            transcendentals=count * rows * half,
        ),
    )(
        tokens,
        routes.T,
        mixing.T,
        gate_weight.reshape(2, width, half),
        up_weight.reshape(2, width, half),
        down_weight.reshape(2, half, width),
    )
    mixed, hessian = pl.pallas_call(
        settle,
        out_shape=(
            jax.ShapeDtypeStruct(mixed.shape, bf16),
            jax.ShapeDtypeStruct(hessian.shape, f32),
        ),
        in_specs=[hbm, hbm],
        out_specs=(hbm, hbm),
        scratch_shapes=[
            pltpu.VMEM(mixed.shape, bf16),
            pltpu.VMEM(hessian.shape, f32),
            dma((2, 5)),
        ],
        compiler_params=pltpu.CompilerParams(vmem_limit_bytes=60 * 2**20),
    )(mixed, hessian)
    return (mixed, hessian[None])


def shards(tokens, routes, mixing, gate_weight, up_weight, down_weight):
    expert_count = lax.axis_size("expert")
    if 2 * routes.shape[1] >= expert_count:
        return gathered(tokens, routes, mixing, gate_weight, up_weight, down_weight)
    return dispatch(tokens, routes, mixing, gate_weight, up_weight, down_weight)


def solution(mesh):
    placed = (
        P("expert", "token"),
        P("expert", None),
        P("expert", None),
        P("expert", None, "token"),
        P("expert", None, "token"),
        P("expert", None, "token"),
    )
    return jax.shard_map(
        shards,
        mesh=mesh,
        in_specs=placed,
        out_specs=(P("expert", "token"), P("expert", "token", None)),
        check_vma=False,
    )
```

```python
import functools
import math

import jax
import jax.numpy as jnp
from jax import lax
from jax.experimental import pallas as pl
from jax.experimental.pallas import tpu as pltpu
from jax.sharding import PartitionSpec as P

MESH = pl.DeviceIdType.MESH
PIECES = 2


def dispatch(tokens, routes, mixing, gate_weight, up_weight, down_weight):
    tok_rows = tokens.shape[0]
    feat_width = tokens.shape[1]
    top_count = routes.shape[1]
    expert_count = lax.axis_size("expert")
    capacity = 2 * tok_rows * top_count // expert_count
    slot_total = expert_count * capacity
    flat_ids = routes.reshape(-1)
    chosen = (flat_ids[:, None] == jnp.arange(expert_count, dtype=jnp.int32)[None, :]).astype(
        jnp.int32
    )
    ranks = jnp.cumsum(chosen, axis=0) - chosen
    slots = jnp.sum(ranks * chosen, axis=1)
    counts = jnp.sum(chosen, axis=0)
    target = flat_ids * capacity + slots
    placing = (target[:, None] == jnp.arange(slot_total, dtype=jnp.int32)[None, :]).astype(
        jnp.bfloat16
    )
    placing = jnp.sum(placing.reshape(tok_rows, top_count, slot_total), axis=1)
    outgoing = lax.dot_general(
        placing, tokens, (((0,), (0,)), ((), ())), preferred_element_type=jnp.float32
    )
    outgoing = outgoing.astype(jnp.bfloat16).reshape(expert_count, capacity, feat_width)
    received, got_counts = (
        lax.all_to_all(outgoing, "expert", split_axis=0, concat_axis=0, tiled=True),
        lax.all_to_all(
            counts.astype(jnp.bfloat16), "expert", split_axis=0, concat_axis=0, tiled=True
        ),
    )
    rows_in = received.reshape(slot_total, feat_width)
    row_total = jnp.sum(got_counts.astype(jnp.float32))
    gate_local = gate_weight[0]
    up_local = up_weight[0]
    piece = lax.all_gather(rows_in, "token", axis=1, tiled=True)
    gate = jnp.dot(piece, gate_local, preferred_element_type=jnp.float32)
    upper = jnp.dot(piece, up_local, preferred_element_type=jnp.float32)
    hidden = (jax.nn.silu(gate) * upper).astype(jnp.bfloat16)
    down_local = down_weight[0]
    piece = lax.all_gather(hidden, "token", axis=1, tiled=True)
    out_sum = jnp.dot(piece, down_local, preferred_element_type=jnp.float32)
    outer = lax.dot_general(
        hidden, piece, (((0,), (0,)), ((), ())), preferred_element_type=jnp.float32
    )
    gram = outer
    out_sum, gram = (out_sum, gram)
    hessian = (2.0 / row_total * gram)[None]
    expert_out = out_sum.astype(jnp.bfloat16).reshape(expert_count, capacity, feat_width)
    returned = lax.all_to_all(expert_out, "expert", split_axis=0, concat_axis=0, tiled=True)
    picked = returned.reshape(slot_total, feat_width)[target]
    picked = picked.reshape(tok_rows, top_count, feat_width).astype(jnp.float32)
    mixed = jnp.sum(picked * mixing[:, :, None], axis=1).astype(jnp.bfloat16)
    return (mixed, hessian)


def exchange(
    side,
    layers,
    tokens_hbm,
    routes_ref,
    mixing_ref,
    gate_hbm,
    up_hbm,
    down_hbm,
    mixed_ref,
    hess_hbm,
    tok,
    table,
    weight,
    gate_v,
    up_v,
    down_v,
    hid,
    part,
    in_b,
    in_a,
    in_z,
    hess_v,
    local_sem,
    tok_send,
    tok_recv,
    tab_send,
    tab_recv,
    pair_send,
    pair_recv,
    hid_send,
    hid_recv,
    back_send,
    back_recv,
    chain_send,
):
    groups = side * side
    rows, width = mixed_ref.shape
    half = gate_v.shape[2]
    me = lax.axis_index("expert")
    core = lax.axis_index("token")
    z, y, x = me // groups, (me // side) % side, me % side
    stride_a = jnp.where(core == 0, side, 1)
    stride_b = jnp.where(core == 0, 1, side)
    pos_a = jnp.where(core == 0, y, x)
    pos_b = jnp.where(core == 0, x, y)

    def peer_z(step):
        return me + ((z + step) % layers - z) * groups

    def peer_a(step):
        return me + ((pos_a + step) % side - pos_a) * stride_a

    def peer_b(step):
        return me + ((pos_b + step) % side - pos_b) * stride_b

    def slot(dz, da, db):
        return (da * stride_a + db * stride_b) * layers + dz

    def label(dz, da, db):
        return (da * side + db) * layers + dz

    def remote(src, dst, send, recv, to, to_core=None):
        return pltpu.make_async_remote_copy(
            src_ref=src,
            dst_ref=dst,
            send_sem=send,
            recv_sem=recv,
            device_id=(to, core if to_core is None else to_core),
            device_id_type=MESH,
        )

    piece = rows // PIECES

    def cut(h):
        return pl.ds(h * piece, piece)

    def forward(dz, da, db, h):
        if db:
            source, to = slot(dz, da, 0), peer_b(db)
        elif da:
            source, to = slot(dz, 0, 0), peer_a(da)
        else:
            source, to = slot(0, 0, 0), peer_z(dz)
        name = label(dz, da, db)
        here = slot(dz, da, db)
        copies = [
            remote(
                tok.at[core, source, cut(h)],
                tok.at[core, here, cut(h)],
                tok_send.at[name, h],
                tok_recv.at[name, h],
                to,
            )
        ]
        if h == 0:
            copies.insert(
                0,
                remote(table.at[source], table.at[here], tab_send.at[name], tab_recv.at[name], to),
            )
        return copies

    def start(copies):
        for copy in copies:
            copy.start()

    def arrive(copies):
        for copy in copies:
            copy.wait_recv()

    def across(where, h):
        return remote(
            tok.at[core, where, cut(h)],
            tok.at[core, where, cut(h)],
            pair_send.at[where, h],
            pair_recv.at[where, h],
            me,
            1 - core,
        )

    def from_pair(where, h):
        return remote(
            tok.at[1 - core, where, cut(h)],
            tok.at[1 - core, where, cut(h)],
            pair_send.at[where, h],
            pair_recv.at[where, h],
            me,
            1 - core,
        )

    loads = [
        pltpu.make_async_copy(tokens_hbm, tok.at[core, 0], local_sem.at[0]),
        pltpu.make_async_copy(gate_hbm, gate_v, local_sem.at[1]),
        pltpu.make_async_copy(up_hbm, up_v, local_sem.at[2]),
        pltpu.make_async_copy(down_hbm, down_v, local_sem.at[3]),
    ]
    start(loads)
    barrier = pltpu.get_barrier_semaphore()
    partners = [(peer_z(d), core) for d in range(1, layers)]
    partners += [(peer_a(d), core) for d in range(1, side)]
    partners += [(peer_b(d), core) for d in range(1, side)]
    partners += [(me, 1 - core)]
    for partner in partners:
        pl.semaphore_signal(barrier, inc=1, device_id=partner, device_id_type=MESH)
    named = lax.broadcasted_iota(jnp.int32, (table.shape[1], rows), 0)
    shares = jnp.zeros((table.shape[1], rows), jnp.float32)
    for k in range(routes_ref.shape[0]):
        shares += jnp.where(routes_ref[k : k + 1, :] == named, mixing_ref[k : k + 1, :], 0.0)
    table[0, :, 0:rows] = shares
    loads[0].wait()
    pl.semaphore_wait(barrier, len(partners))

    orders = [
        sorted(range(1, layers), key=lambda d: (d if d <= place else layers - d, d))
        for place in range(layers)
    ]

    def coming(k):
        return sum(jnp.where(z == place, orders[place][k], 0) for place in range(layers))

    def chain(s, way, here, h):
        source = slot(s, 0, 0)
        there = slot(here, 0, 0)
        to = me + (groups if way == 0 else -groups)
        copies = [
            remote(
                tok.at[core, source, cut(h)],
                tok.at[core, there, cut(h)],
                chain_send.at[way, s, h],
                tok_recv.at[here, h],
                to,
            )
        ]
        if h == 0:
            copies.insert(
                0,
                remote(
                    table.at[source],
                    table.at[there],
                    chain_send.at[2 + way, s, 0],
                    tab_recv.at[here],
                    to,
                ),
            )
        return copies

    def along(s, h, act):
        @pl.when((z < layers - 1) & (s <= z))
        def _():
            for copy in chain(s, 0, s + 1, h):
                act(copy)

        @pl.when((z > 0) & ((s == 0) | (s > z)))
        def _():
            for copy in chain(s, 1, (s + layers - 1) % layers, h):
                act(copy)

    def spread(dz, h):
        along(dz, h, lambda copy: copy.start())
        for d in range(1, side):
            start(forward(dz, d, 0, h))
            start(forward(dz, 0, d, h))
        across(slot(dz, 0, 0), h).start()

    def turn(dz, h):
        for da in range(1, side):
            arrive(forward(dz, da, 0, h))
            for db in range(1, side):
                start(forward(dz, da, db, h))
            across(slot(dz, da, 0), h).start()

    def straight(dz, h):
        for db in range(1, side):
            arrive(forward(dz, 0, db, h))
            across(slot(dz, 0, db), h).start()

    def last(dz, h):
        for da in range(1, side):
            for db in range(1, side):
                arrive(forward(dz, da, db, h))
                across(slot(dz, da, db), h).start()

    sequence = [0] + [coming(k) for k in range(layers - 1)]
    for h in range(PIECES):
        spread(sequence[0], h)
    for k in range(1, layers):
        for h in range(PIECES):
            arrive(forward(sequence[k], 0, 0, h))
            spread(sequence[k], h)
            turn(sequence[k - 1], h)
        for h in range(PIECES):
            straight(sequence[k - 1], h)
    for h in range(PIECES):
        turn(sequence[-1], h)

    tall = layers * rows
    tile = min(256, half)
    diagonal = lax.broadcasted_iota(jnp.int32, (rows, rows), 0) == lax.broadcasted_iota(
        jnp.int32, (rows, rows), 1
    )

    def row_weights(span, count):
        wide = weight[span].reshape(count, weight.shape[2])
        return jnp.concatenate([wide] * (tile // weight.shape[2]), axis=1)

    def up_project(g, many=1):
        first = g * layers
        blocks = many * layers
        tall = blocks * rows
        span = pl.ds(first, blocks)
        for i in range(blocks):
            for h in range(PIECES):
                from_pair(first + i, h).wait_recv()
            mine = table[first + i, pl.ds(me, 1), 0:rows]
            column = jnp.sum(jnp.where(diagonal, mine, 0.0), axis=1, keepdims=True)
            weight[first + i] = jnp.broadcast_to(column, weight.shape[1:])

        @pl.loop(0, half // tile)
        def _(j):
            cols = pl.ds(pl.multiple_of(j * tile, tile), tile)
            left = tok[0, span].reshape(tall, width)
            right = tok[1, span].reshape(tall, width)
            gate = jnp.dot(left, gate_v[0, :, cols], preferred_element_type=jnp.float32)
            gate += jnp.dot(right, gate_v[1, :, cols], preferred_element_type=jnp.float32)
            upper = jnp.dot(left, up_v[0, :, cols], preferred_element_type=jnp.float32)
            upper += jnp.dot(right, up_v[1, :, cols], preferred_element_type=jnp.float32)
            chosen = row_weights(span, tall) > 0
            value = gate / (1.0 + jnp.exp(-gate)) * upper
            value = jnp.where(chosen, value, 0.0).astype(jnp.bfloat16)
            hid[core, span, :, cols] = value.reshape(blocks, rows, tile)

        for each in range(g, g + many):
            hidden_copy(each).start()

    def hidden_copy(g):
        span = pl.ds(g * layers, layers)
        return remote(
            hid.at[core, span],
            hid.at[core, span],
            hid_send.at[g],
            hid_recv.at[g],
            me,
            1 - core,
        )

    def hidden_from_pair(g):
        span = pl.ds(g * layers, layers)
        return remote(
            hid.at[1 - core, span],
            hid.at[1 - core, span],
            hid_send.at[g],
            hid_recv.at[g],
            me,
            1 - core,
        )

    def down_project(g):
        span = pl.ds(g * layers, layers)
        hidden_from_pair(g).wait_recv()

        @pl.loop(0, width // tile)
        def _(j):
            cols = pl.ds(pl.multiple_of(j * tile, tile), tile)
            left = hid[0, span].reshape(tall, half)
            right = hid[1, span].reshape(tall, half)
            out = jnp.dot(left, down_v[0, :, cols], preferred_element_type=jnp.float32)
            out += jnp.dot(right, down_v[1, :, cols], preferred_element_type=jnp.float32)
            out *= row_weights(span, tall)
            part[span, :, cols] = out.astype(jnp.bfloat16).reshape(layers, rows, tile)

    def back(dz, da, db, h):
        name = label(dz, da, db)
        source = part.at[slot(dz, da, db), cut(h)]
        if db:
            target, to = in_b.at[db - 1, da * layers + dz, cut(h)], peer_b(side - db)
        elif da:
            target, to = in_a.at[da - 1, dz, cut(h)], peer_a(side - da)
        else:
            target, to = in_z.at[dz - 1, cut(h)], peer_z(layers - dz)
        return remote(source, target, back_send.at[name, h], back_recv.at[name, h], to)

    def summed(dz, da, h):
        total = part[slot(dz, da, 0), cut(h)].astype(jnp.float32)
        for db in range(1, side):
            back(dz, da, db, h).wait_recv()
            total += in_b[db - 1, da * layers + dz, cut(h)].astype(jnp.float32)
        if da == 0:
            for d in range(1, side):
                back(dz, d, 0, h).wait_recv()
                total += in_a[d - 1, dz, cut(h)].astype(jnp.float32)
        return total

    far = sorted(range(1, layers), key=lambda d: -min(d, layers - d))

    def send_back(da, db):
        for dz in far + [0]:
            for h in range(PIECES):
                back(dz, da, db, h).start()

    for load in loads[1:]:
        load.wait()
    up_project(0)
    for h in range(PIECES):
        straight(sequence[-1], h)
    edge = [g for g in range(1, groups) if g // side == 0 or g % side == 0]
    inner = [g for g in range(1, groups) if g not in edge]
    if edge == list(range(edge[0], edge[-1] + 1)):
        up_project(edge[0], len(edge))
    else:
        for g in edge:
            up_project(g)
    for k in range(layers):
        for h in range(PIECES):
            last(sequence[k], h)
    for db in range(1, side):
        down_project(db * stride_b)
        send_back(0, db)
    for g in inner:
        up_project(g)
    for da in range(1, side):
        down_project(da * stride_a)
    for da in range(1, side):
        for db in range(1, side):
            down_project(da * stride_a + db * stride_b)
            send_back(da, db)
    down_project(0)

    named_rows = jnp.zeros((rows, weight.shape[2]), jnp.float32)
    for s in range(weight.shape[0]):
        named_rows += (weight[s] > 0).astype(jnp.float32)
    count = jnp.sum(named_rows, axis=0, keepdims=True)[:, 0:1]
    scale = 2.0 / count
    every = weight.shape[0] * rows

    def hessian_half(h):
        @pl.loop(0, half // tile)
        def _(j):
            cols = pl.ds(pl.multiple_of(j * tile, tile), tile)
            gram = lax.dot_general(
                hid[core, :, :, cols].reshape(every, tile),
                hid[h].reshape(every, half),
                (((0,), (0,)), ((), ())),
                preferred_element_type=jnp.float32,
            )
            hess_v[cols, pl.ds(h * half, half)] = gram * scale

    hessian_half(0)
    for da in range(1, side):
        for dz in far + [0]:
            for h in range(PIECES):
                part[slot(dz, da, 0), cut(h)] = summed(dz, da, h).astype(jnp.bfloat16)
                back(dz, da, 0, h).start()
    hessian_half(1)
    store = pltpu.make_async_copy(hess_v, hess_hbm, local_sem.at[0])
    store.start()
    for dz in far:
        for h in range(PIECES):
            part[dz, cut(h)] = summed(dz, 0, h).astype(jnp.bfloat16)
            back(dz, 0, 0, h).start()
    for h in range(PIECES):
        total = summed(0, 0, h)
        for dz in far:
            back(dz, 0, 0, h).wait_recv()
            total += in_z[dz - 1, cut(h)].astype(jnp.float32)
        mixed_ref[cut(h)] = total.astype(jnp.bfloat16)

    store.wait()
    for h in range(PIECES):
        for da in range(side):
            for db in range(side):
                for dz in range(layers):
                    across(slot(dz, da, db), h).wait_send()
                    if da or db:
                        for copy in forward(dz, da, db, h):
                            copy.wait_send()
                    if dz or da or db:
                        back(dz, da, db, h).wait_send()
        for dz in range(layers):
            along(dz, h, lambda copy: copy.wait_send())
    for g in range(groups):
        hidden_copy(g).wait_send()


def settle(mixed_in, hess_in, mixed_out, hess_out, mixed_v, hess_v, sems):
    pieces = 4
    span = hess_in.shape[0] // pieces
    moves = [(mixed_in, mixed_v, mixed_out)]
    for i in range(pieces):
        moves.append([ref.at[pl.ds(i * span, span)] for ref in (hess_in, hess_v, hess_out)])
    comes = [pltpu.make_async_copy(m[0], m[1], sems.at[0, i]) for i, m in enumerate(moves)]
    goes = [pltpu.make_async_copy(m[1], m[2], sems.at[1, i]) for i, m in enumerate(moves)]
    for copy in comes:
        copy.start()
    for come, go in zip(comes, goes):
        come.wait()
        go.start()
    for go in goes:
        go.wait()


def gathered(tokens, routes, mixing, gate_weight, up_weight, down_weight):
    count = lax.axis_size("expert")
    side = math.isqrt(count // 4)
    layers = count // (side * side)
    rows, width = tokens.shape
    depth, half = gate_weight.shape[1:]
    lanes = -(-rows // 128) * 128
    bf16, f32 = jnp.bfloat16, jnp.float32
    dma = pltpu.SemaphoreType.DMA
    hbm = pl.BlockSpec(memory_space=pl.ANY)
    vmem = pl.BlockSpec(memory_space=pltpu.VMEM)
    flops = 2 * count * rows * (2 * depth * half + 2 * half * width + 2 * half * half)
    mixed, hessian = pl.pallas_call(
        functools.partial(exchange, side, layers),
        out_shape=(
            jax.ShapeDtypeStruct((rows, width), bf16),
            jax.ShapeDtypeStruct((half, 2 * half), f32),
        ),
        in_specs=[hbm, vmem, vmem, hbm, hbm, hbm],
        out_specs=(vmem, hbm),
        scratch_shapes=[
            pltpu.VMEM((2, count, rows, width), bf16),
            pltpu.VMEM((count, count, lanes), f32),
            pltpu.VMEM((count, rows, 128), f32),
            pltpu.VMEM((2, width, half), bf16),
            pltpu.VMEM((2, width, half), bf16),
            pltpu.VMEM((2, half, width), bf16),
            pltpu.VMEM((2, count, rows, half), bf16),
            pltpu.VMEM((count, rows, width), bf16),
            pltpu.VMEM((side - 1, side * layers, rows, width), bf16),
            pltpu.VMEM((side - 1, layers, rows, width), bf16),
            pltpu.VMEM((layers - 1, rows, width), bf16),
            pltpu.VMEM((half, 2 * half), f32),
            dma((4,)),
            dma((count, PIECES)),
            dma((count, PIECES)),
            dma((count,)),
            dma((count,)),
            dma((count, PIECES)),
            dma((count, PIECES)),
            dma((side * side,)),
            dma((side * side,)),
            dma((count, PIECES)),
            dma((count, PIECES)),
            dma((4, layers, PIECES)),
        ],
        compiler_params=pltpu.CompilerParams(
            collective_id=0, has_side_effects=True, vmem_limit_bytes=60 * 2**20
        ),
        cost_estimate=pl.CostEstimate(
            flops=flops,
            bytes_accessed=2 * (2 * depth * half + 2 * half * width),
            transcendentals=count * rows * half,
        ),
    )(
        tokens,
        routes.T,
        mixing.T,
        gate_weight.reshape(2, width, half),
        up_weight.reshape(2, width, half),
        down_weight.reshape(2, half, width),
    )
    mixed, hessian = pl.pallas_call(
        settle,
        out_shape=(
            jax.ShapeDtypeStruct(mixed.shape, bf16),
            jax.ShapeDtypeStruct(hessian.shape, f32),
        ),
        in_specs=[hbm, hbm],
        out_specs=(hbm, hbm),
        scratch_shapes=[
            pltpu.VMEM(mixed.shape, bf16),
            pltpu.VMEM(hessian.shape, f32),
            dma((2, 5)),
        ],
        compiler_params=pltpu.CompilerParams(vmem_limit_bytes=60 * 2**20),
    )(mixed, hessian)
    return (mixed, hessian[None])


def shards(tokens, routes, mixing, gate_weight, up_weight, down_weight):
    expert_count = lax.axis_size("expert")
    if 2 * routes.shape[1] >= expert_count:
        return gathered(tokens, routes, mixing, gate_weight, up_weight, down_weight)
    return dispatch(tokens, routes, mixing, gate_weight, up_weight, down_weight)


def solution(mesh):
    placed = (
        P("expert", "token"),
        P("expert", None),
        P("expert", None),
        P("expert", None, "token"),
        P("expert", None, "token"),
        P("expert", None, "token"),
    )
    return jax.shard_map(
        shards,
        mesh=mesh,
        in_specs=placed,
        out_specs=(P("expert", "token"), P("expert", "token", None)),
        check_vma=False,
    )
```

```python
import functools
import math

import jax
import jax.numpy as jnp
from jax import lax
from jax.experimental import pallas as pl
from jax.experimental.pallas import tpu as pltpu
from jax.sharding import PartitionSpec as P

MESH = pl.DeviceIdType.MESH


def dispatch(tokens, routes, mixing, gate_weight, up_weight, down_weight):
    tok_rows = tokens.shape[0]
    feat_width = tokens.shape[1]
    top_count = routes.shape[1]
    expert_count = lax.axis_size("expert")
    capacity = 2 * tok_rows * top_count // expert_count
    slot_total = expert_count * capacity
    flat_ids = routes.reshape(-1)
    chosen = (flat_ids[:, None] == jnp.arange(expert_count, dtype=jnp.int32)[None, :]).astype(
        jnp.int32
    )
    ranks = jnp.cumsum(chosen, axis=0) - chosen
    slots = jnp.sum(ranks * chosen, axis=1)
    counts = jnp.sum(chosen, axis=0)
    target = flat_ids * capacity + slots
    placing = (target[:, None] == jnp.arange(slot_total, dtype=jnp.int32)[None, :]).astype(
        jnp.bfloat16
    )
    placing = jnp.sum(placing.reshape(tok_rows, top_count, slot_total), axis=1)
    outgoing = lax.dot_general(
        placing, tokens, (((0,), (0,)), ((), ())), preferred_element_type=jnp.float32
    )
    outgoing = outgoing.astype(jnp.bfloat16).reshape(expert_count, capacity, feat_width)
    received, got_counts = (
        lax.all_to_all(outgoing, "expert", split_axis=0, concat_axis=0, tiled=True),
        lax.all_to_all(
            counts.astype(jnp.bfloat16), "expert", split_axis=0, concat_axis=0, tiled=True
        ),
    )
    rows_in = received.reshape(slot_total, feat_width)
    row_total = jnp.sum(got_counts.astype(jnp.float32))
    gate_local = gate_weight[0]
    up_local = up_weight[0]
    piece = lax.all_gather(rows_in, "token", axis=1, tiled=True)
    gate = jnp.dot(piece, gate_local, preferred_element_type=jnp.float32)
    upper = jnp.dot(piece, up_local, preferred_element_type=jnp.float32)
    hidden = (jax.nn.silu(gate) * upper).astype(jnp.bfloat16)
    down_local = down_weight[0]
    piece = lax.all_gather(hidden, "token", axis=1, tiled=True)
    out_sum = jnp.dot(piece, down_local, preferred_element_type=jnp.float32)
    outer = lax.dot_general(
        hidden, piece, (((0,), (0,)), ((), ())), preferred_element_type=jnp.float32
    )
    gram = outer
    out_sum, gram = (out_sum, gram)
    hessian = (2.0 / row_total * gram)[None]
    expert_out = out_sum.astype(jnp.bfloat16).reshape(expert_count, capacity, feat_width)
    returned = lax.all_to_all(expert_out, "expert", split_axis=0, concat_axis=0, tiled=True)
    picked = returned.reshape(slot_total, feat_width)[target]
    picked = picked.reshape(tok_rows, top_count, feat_width).astype(jnp.float32)
    mixed = jnp.sum(picked * mixing[:, :, None], axis=1).astype(jnp.bfloat16)
    return (mixed, hessian)


def exchange(
    side,
    layers,
    tokens_hbm,
    routes_ref,
    mixing_ref,
    gate_hbm,
    up_hbm,
    down_hbm,
    mixed_ref,
    hess_hbm,
    tok,
    table,
    weight,
    gate_v,
    up_v,
    down_v,
    hid,
    part,
    in_b,
    in_a,
    in_z,
    hess_v,
    local_sem,
    tok_send,
    tok_recv,
    tab_send,
    tab_recv,
    pair_send,
    pair_recv,
    hid_send,
    hid_recv,
    back_send,
    back_recv,
    chain_send,
):
    groups = side * side
    rows, width = mixed_ref.shape
    half = gate_v.shape[2]
    me = lax.axis_index("expert")
    core = lax.axis_index("token")
    z, y, x = me // groups, (me // side) % side, me % side
    stride_a = jnp.where(core == 0, side, 1)
    stride_b = jnp.where(core == 0, 1, side)
    pos_a = jnp.where(core == 0, y, x)
    pos_b = jnp.where(core == 0, x, y)

    def peer_z(step):
        return me + ((z + step) % layers - z) * groups

    def peer_a(step):
        return me + ((pos_a + step) % side - pos_a) * stride_a

    def peer_b(step):
        return me + ((pos_b + step) % side - pos_b) * stride_b

    def slot(dz, da, db):
        return (da * stride_a + db * stride_b) * layers + dz

    def label(dz, da, db):
        return (da * side + db) * layers + dz

    def remote(src, dst, send, recv, to, to_core=None):
        return pltpu.make_async_remote_copy(
            src_ref=src,
            dst_ref=dst,
            send_sem=send,
            recv_sem=recv,
            device_id=(to, core if to_core is None else to_core),
            device_id_type=MESH,
        )

    def forward(dz, da, db):
        if db:
            source, to = slot(dz, da, 0), peer_b(db)
        elif da:
            source, to = slot(dz, 0, 0), peer_a(da)
        else:
            source, to = slot(0, 0, 0), peer_z(dz)
        name = label(dz, da, db)
        here = slot(dz, da, db)
        return (
            remote(table.at[source], table.at[here], tab_send.at[name], tab_recv.at[name], to),
            remote(
                tok.at[core, source],
                tok.at[core, here],
                tok_send.at[name],
                tok_recv.at[name],
                to,
            ),
        )

    def start(copies):
        for copy in copies:
            copy.start()

    def arrive(copies):
        for copy in copies:
            copy.wait_recv()

    def across(where):
        return remote(
            tok.at[core, where],
            tok.at[core, where],
            pair_send.at[where],
            pair_recv.at[where],
            me,
            1 - core,
        )

    def from_pair(where):
        return remote(
            tok.at[1 - core, where],
            tok.at[1 - core, where],
            pair_send.at[where],
            pair_recv.at[where],
            me,
            1 - core,
        )

    loads = [
        pltpu.make_async_copy(tokens_hbm, tok.at[core, 0], local_sem.at[0]),
        pltpu.make_async_copy(gate_hbm, gate_v, local_sem.at[1]),
        pltpu.make_async_copy(up_hbm, up_v, local_sem.at[2]),
        pltpu.make_async_copy(down_hbm, down_v, local_sem.at[3]),
    ]
    start(loads)
    barrier = pltpu.get_barrier_semaphore()
    partners = [(peer_z(d), core) for d in range(1, layers)]
    partners += [(peer_a(d), core) for d in range(1, side)]
    partners += [(peer_b(d), core) for d in range(1, side)]
    partners += [(me, 1 - core)]
    for partner in partners:
        pl.semaphore_signal(barrier, inc=1, device_id=partner, device_id_type=MESH)
    named = lax.broadcasted_iota(jnp.int32, (table.shape[1], rows), 0)
    shares = jnp.zeros((table.shape[1], rows), jnp.float32)
    for k in range(routes_ref.shape[0]):
        shares += jnp.where(routes_ref[k : k + 1, :] == named, mixing_ref[k : k + 1, :], 0.0)
    table[0, :, 0:rows] = shares
    loads[0].wait()
    pl.semaphore_wait(barrier, len(partners))

    orders = [
        sorted(range(1, layers), key=lambda d: (d if d <= place else layers - d, d))
        for place in range(layers)
    ]

    def coming(k):
        return sum(jnp.where(z == place, orders[place][k], 0) for place in range(layers))

    def chain(s, way, here):
        source = slot(s, 0, 0)
        there = slot(here, 0, 0)
        to = me + (groups if way == 0 else -groups)
        return (
            remote(
                table.at[source],
                table.at[there],
                chain_send.at[2 + way, s],
                tab_recv.at[here],
                to,
            ),
            remote(
                tok.at[core, source],
                tok.at[core, there],
                chain_send.at[way, s],
                tok_recv.at[here],
                to,
            ),
        )

    def along(s, act):
        @pl.when((z < layers - 1) & (s <= z))
        def _():
            for copy in chain(s, 0, s + 1):
                act(copy)

        @pl.when((z > 0) & ((s == 0) | (s > z)))
        def _():
            for copy in chain(s, 1, (s + layers - 1) % layers):
                act(copy)

    def spread(dz):
        along(dz, lambda copy: copy.start())
        for d in range(1, side):
            start(forward(dz, d, 0))
            start(forward(dz, 0, d))
        across(slot(dz, 0, 0)).start()

    def turn(dz):
        for da in range(1, side):
            arrive(forward(dz, da, 0))
            for db in range(1, side):
                start(forward(dz, da, db))
            across(slot(dz, da, 0)).start()

    def straight(dz):
        for db in range(1, side):
            arrive(forward(dz, 0, db))
            across(slot(dz, 0, db)).start()

    def last(dz):
        for da in range(1, side):
            for db in range(1, side):
                arrive(forward(dz, da, db))
                across(slot(dz, da, db)).start()

    sequence = [0] + [coming(k) for k in range(layers - 1)]
    spread(sequence[0])
    for k in range(1, layers):
        arrive(forward(sequence[k], 0, 0))
        spread(sequence[k])
        turn(sequence[k - 1])
        straight(sequence[k - 1])
    turn(sequence[-1])

    tall = layers * rows
    tile = min(256, half)
    diagonal = lax.broadcasted_iota(jnp.int32, (rows, rows), 0) == lax.broadcasted_iota(
        jnp.int32, (rows, rows), 1
    )

    def row_weights(span, count):
        wide = weight[span].reshape(count, weight.shape[2])
        return jnp.concatenate([wide] * (tile // weight.shape[2]), axis=1)

    def up_project(g, many=1, between=None):
        first = g * layers
        blocks = many * layers
        tall = blocks * rows
        span = pl.ds(first, blocks)
        for i in range(blocks):
            from_pair(first + i).wait_recv()
            mine = table[first + i, pl.ds(me, 1), 0:rows]
            column = jnp.sum(jnp.where(diagonal, mine, 0.0), axis=1, keepdims=True)
            weight[first + i] = jnp.broadcast_to(column, weight.shape[1:])

        for j in range(half // tile):
            cols = pl.ds(j * tile, tile)
            left = tok[0, span].reshape(tall, width)
            right = tok[1, span].reshape(tall, width)
            gate = jnp.dot(left, gate_v[0, :, cols], preferred_element_type=jnp.float32)
            gate += jnp.dot(right, gate_v[1, :, cols], preferred_element_type=jnp.float32)
            upper = jnp.dot(left, up_v[0, :, cols], preferred_element_type=jnp.float32)
            upper += jnp.dot(right, up_v[1, :, cols], preferred_element_type=jnp.float32)
            chosen = row_weights(span, tall) > 0
            value = gate / (1.0 + jnp.exp(-gate)) * upper
            value = jnp.where(chosen, value, 0.0).astype(jnp.bfloat16)
            hid[core, span, :, cols] = value.reshape(blocks, rows, tile)
            if between is not None:
                between(j)

        for each in range(g, g + many):
            hidden_copy(each).start()

    def hidden_copy(g):
        span = pl.ds(g * layers, layers)
        return remote(
            hid.at[core, span],
            hid.at[core, span],
            hid_send.at[g],
            hid_recv.at[g],
            me,
            1 - core,
        )

    def hidden_from_pair(g):
        span = pl.ds(g * layers, layers)
        return remote(
            hid.at[1 - core, span],
            hid.at[1 - core, span],
            hid_send.at[g],
            hid_recv.at[g],
            me,
            1 - core,
        )

    def down_project(g):
        span = pl.ds(g * layers, layers)
        hidden_from_pair(g).wait_recv()

        @pl.loop(0, width // tile)
        def _(j):
            cols = pl.ds(pl.multiple_of(j * tile, tile), tile)
            left = hid[0, span].reshape(tall, half)
            right = hid[1, span].reshape(tall, half)
            out = jnp.dot(left, down_v[0, :, cols], preferred_element_type=jnp.float32)
            out += jnp.dot(right, down_v[1, :, cols], preferred_element_type=jnp.float32)
            out *= row_weights(span, tall)
            part[span, :, cols] = out.astype(jnp.bfloat16).reshape(layers, rows, tile)

    def back(dz, da, db):
        name = label(dz, da, db)
        source = part.at[slot(dz, da, db)]
        if db:
            target, to = in_b.at[db - 1, da * layers + dz], peer_b(side - db)
        elif da:
            target, to = in_a.at[da - 1, dz], peer_a(side - da)
        else:
            target, to = in_z.at[dz - 1], peer_z(layers - dz)
        return remote(source, target, back_send.at[name], back_recv.at[name], to)

    def summed(dz, da):
        total = part[slot(dz, da, 0)].astype(jnp.float32)
        for db in range(1, side):
            back(dz, da, db).wait_recv()
            total += in_b[db - 1, da * layers + dz].astype(jnp.float32)
        if da == 0:
            for d in range(1, side):
                back(dz, d, 0).wait_recv()
                total += in_a[d - 1, dz].astype(jnp.float32)
        return total

    far = sorted(range(1, layers), key=lambda d: -min(d, layers - d))

    def send_back(da, db):
        for dz in far + [0]:
            back(dz, da, db).start()

    for load in loads[1:]:
        load.wait()
    up_project(0)
    straight(sequence[-1])
    edge = [g for g in range(1, groups) if g // side == 0 or g % side == 0]
    inner = [g for g in range(1, groups) if g not in edge]
    down_project(0)
    share = layers // (half // tile)

    def pass_on(j):
        for k in range(j * share, j * share + share):
            last(sequence[k])

    if edge == list(range(edge[0], edge[-1] + 1)) and share * (half // tile) == layers:
        up_project(edge[0], len(edge), pass_on)
    else:
        for g in edge:
            up_project(g)
        for k in range(layers):
            last(sequence[k])
    for db in range(1, side):
        down_project(db * stride_b)
        send_back(0, db)
    for g in inner:
        up_project(g)
    for da in range(1, side):
        down_project(da * stride_a)
    for da in range(1, side):
        for db in range(1, side):
            down_project(da * stride_a + db * stride_b)
            send_back(da, db)

    named_rows = jnp.zeros((rows, weight.shape[2]), jnp.float32)
    for s in range(weight.shape[0]):
        named_rows += (weight[s] > 0).astype(jnp.float32)
    count = jnp.sum(named_rows, axis=0, keepdims=True)[:, 0:1]
    scale = 2.0 / count
    every = weight.shape[0] * rows

    def hessian_tile(h, j):
        cols = pl.ds(j * tile, tile)
        gram = lax.dot_general(
            hid[core, :, :, cols].reshape(every, tile),
            hid[h].reshape(every, half),
            (((0,), (0,)), ((), ())),
            preferred_element_type=jnp.float32,
        )
        hess_v[cols, pl.ds(h * half, half)] = gram * scale

    tiles = [(h, j) for h in range(2) for j in range(half // tile)]
    for da in range(1, side):
        for dz in far + [0]:
            part[slot(dz, da, 0)] = summed(dz, da).astype(jnp.bfloat16)
            back(dz, da, 0).start()
            if tiles:
                hessian_tile(*tiles.pop(0))
    for rest in tiles:
        hessian_tile(*rest)
    store = pltpu.make_async_copy(hess_v, hess_hbm, local_sem.at[0])
    store.start()
    for dz in far:
        part[dz] = summed(dz, 0).astype(jnp.bfloat16)
        back(dz, 0, 0).start()
    total = summed(0, 0)
    for dz in range(1, layers):
        back(dz, 0, 0).wait_recv()
        total += in_z[dz - 1].astype(jnp.float32)
    mixed_ref[...] = total.astype(jnp.bfloat16)

    store.wait()
    for da in range(side):
        for db in range(side):
            for dz in range(layers):
                across(slot(dz, da, db)).wait_send()
                if da or db:
                    for copy in forward(dz, da, db):
                        copy.wait_send()
                if dz or da or db:
                    back(dz, da, db).wait_send()
    for dz in range(layers):
        along(dz, lambda copy: copy.wait_send())
    for g in range(groups):
        hidden_copy(g).wait_send()


def settle(mixed_in, hess_in, mixed_out, hess_out, mixed_v, hess_v, sems):
    pieces = 4
    span = hess_in.shape[0] // pieces
    moves = [(mixed_in, mixed_v, mixed_out)]
    for i in range(pieces):
        moves.append([ref.at[pl.ds(i * span, span)] for ref in (hess_in, hess_v, hess_out)])
    comes = [pltpu.make_async_copy(m[0], m[1], sems.at[0, i]) for i, m in enumerate(moves)]
    goes = [pltpu.make_async_copy(m[1], m[2], sems.at[1, i]) for i, m in enumerate(moves)]
    for copy in comes:
        copy.start()
    for come, go in zip(comes, goes):
        come.wait()
        go.start()
    for go in goes:
        go.wait()


def gathered(tokens, routes, mixing, gate_weight, up_weight, down_weight):
    count = lax.axis_size("expert")
    side = math.isqrt(count // 4)
    layers = count // (side * side)
    rows, width = tokens.shape
    depth, half = gate_weight.shape[1:]
    lanes = -(-rows // 128) * 128
    bf16, f32 = jnp.bfloat16, jnp.float32
    dma = pltpu.SemaphoreType.DMA
    hbm = pl.BlockSpec(memory_space=pl.ANY)
    vmem = pl.BlockSpec(memory_space=pltpu.VMEM)
    flops = 2 * count * rows * (2 * depth * half + 2 * half * width + 2 * half * half)
    mixed, hessian = pl.pallas_call(
        functools.partial(exchange, side, layers),
        out_shape=(
            jax.ShapeDtypeStruct((rows, width), bf16),
            jax.ShapeDtypeStruct((half, 2 * half), f32),
        ),
        in_specs=[hbm, vmem, vmem, hbm, hbm, hbm],
        out_specs=(vmem, hbm),
        scratch_shapes=[
            pltpu.VMEM((2, count, rows, width), bf16),
            pltpu.VMEM((count, count, lanes), f32),
            pltpu.VMEM((count, rows, 128), f32),
            pltpu.VMEM((2, width, half), bf16),
            pltpu.VMEM((2, width, half), bf16),
            pltpu.VMEM((2, half, width), bf16),
            pltpu.VMEM((2, count, rows, half), bf16),
            pltpu.VMEM((count, rows, width), bf16),
            pltpu.VMEM((side - 1, side * layers, rows, width), bf16),
            pltpu.VMEM((side - 1, layers, rows, width), bf16),
            pltpu.VMEM((layers - 1, rows, width), bf16),
            pltpu.VMEM((half, 2 * half), f32),
            dma((4,)),
            dma((count,)),
            dma((count,)),
            dma((count,)),
            dma((count,)),
            dma((count,)),
            dma((count,)),
            dma((side * side,)),
            dma((side * side,)),
            dma((count,)),
            dma((count,)),
            dma((4, layers)),
        ],
        compiler_params=pltpu.CompilerParams(
            collective_id=0, has_side_effects=True, vmem_limit_bytes=60 * 2**20
        ),
        cost_estimate=pl.CostEstimate(
            flops=flops,
            bytes_accessed=2 * (2 * depth * half + 2 * half * width),
            transcendentals=count * rows * half,
        ),
    )(
        tokens,
        routes.T,
        mixing.T,
        gate_weight.reshape(2, width, half),
        up_weight.reshape(2, width, half),
        down_weight.reshape(2, half, width),
    )
    mixed, hessian = pl.pallas_call(
        settle,
        out_shape=(
            jax.ShapeDtypeStruct(mixed.shape, bf16),
            jax.ShapeDtypeStruct(hessian.shape, f32),
        ),
        in_specs=[hbm, hbm],
        out_specs=(hbm, hbm),
        scratch_shapes=[
            pltpu.VMEM(mixed.shape, bf16),
            pltpu.VMEM(hessian.shape, f32),
            dma((2, 5)),
        ],
        compiler_params=pltpu.CompilerParams(vmem_limit_bytes=60 * 2**20),
    )(mixed, hessian)
    return (mixed, hessian[None])


def shards(tokens, routes, mixing, gate_weight, up_weight, down_weight):
    expert_count = lax.axis_size("expert")
    if 2 * routes.shape[1] >= expert_count:
        return gathered(tokens, routes, mixing, gate_weight, up_weight, down_weight)
    return dispatch(tokens, routes, mixing, gate_weight, up_weight, down_weight)


def solution(mesh):
    placed = (
        P("expert", "token"),
        P("expert", None),
        P("expert", None),
        P("expert", None, "token"),
        P("expert", None, "token"),
        P("expert", None, "token"),
    )
    return jax.shard_map(
        shards,
        mesh=mesh,
        in_specs=placed,
        out_specs=(P("expert", "token"), P("expert", "token", None)),
        check_vma=False,
    )
```

```python
import functools
import math

import jax
import jax.numpy as jnp
from jax import lax
from jax.experimental import pallas as pl
from jax.experimental.pallas import tpu as pltpu
from jax.sharding import PartitionSpec as P

MESH = pl.DeviceIdType.MESH


def dispatch(tokens, routes, mixing, gate_weight, up_weight, down_weight):
    tok_rows = tokens.shape[0]
    feat_width = tokens.shape[1]
    top_count = routes.shape[1]
    expert_count = lax.axis_size("expert")
    capacity = 2 * tok_rows * top_count // expert_count
    slot_total = expert_count * capacity
    flat_ids = routes.reshape(-1)
    chosen = (flat_ids[:, None] == jnp.arange(expert_count, dtype=jnp.int32)[None, :]).astype(
        jnp.int32
    )
    ranks = jnp.cumsum(chosen, axis=0) - chosen
    slots = jnp.sum(ranks * chosen, axis=1)
    counts = jnp.sum(chosen, axis=0)
    target = flat_ids * capacity + slots
    placing = (target[:, None] == jnp.arange(slot_total, dtype=jnp.int32)[None, :]).astype(
        jnp.bfloat16
    )
    placing = jnp.sum(placing.reshape(tok_rows, top_count, slot_total), axis=1)
    outgoing = lax.dot_general(
        placing, tokens, (((0,), (0,)), ((), ())), preferred_element_type=jnp.float32
    )
    outgoing = outgoing.astype(jnp.bfloat16).reshape(expert_count, capacity, feat_width)
    received, got_counts = (
        lax.all_to_all(outgoing, "expert", split_axis=0, concat_axis=0, tiled=True),
        lax.all_to_all(
            counts.astype(jnp.bfloat16), "expert", split_axis=0, concat_axis=0, tiled=True
        ),
    )
    rows_in = received.reshape(slot_total, feat_width)
    row_total = jnp.sum(got_counts.astype(jnp.float32))
    gate_local = gate_weight[0]
    up_local = up_weight[0]
    piece = lax.all_gather(rows_in, "token", axis=1, tiled=True)
    gate = jnp.dot(piece, gate_local, preferred_element_type=jnp.float32)
    upper = jnp.dot(piece, up_local, preferred_element_type=jnp.float32)
    hidden = (jax.nn.silu(gate) * upper).astype(jnp.bfloat16)
    down_local = down_weight[0]
    piece = lax.all_gather(hidden, "token", axis=1, tiled=True)
    out_sum = jnp.dot(piece, down_local, preferred_element_type=jnp.float32)
    outer = lax.dot_general(
        hidden, piece, (((0,), (0,)), ((), ())), preferred_element_type=jnp.float32
    )
    gram = outer
    out_sum, gram = (out_sum, gram)
    hessian = (2.0 / row_total * gram)[None]
    expert_out = out_sum.astype(jnp.bfloat16).reshape(expert_count, capacity, feat_width)
    returned = lax.all_to_all(expert_out, "expert", split_axis=0, concat_axis=0, tiled=True)
    picked = returned.reshape(slot_total, feat_width)[target]
    picked = picked.reshape(tok_rows, top_count, feat_width).astype(jnp.float32)
    mixed = jnp.sum(picked * mixing[:, :, None], axis=1).astype(jnp.bfloat16)
    return (mixed, hessian)


def exchange(
    side,
    layers,
    tokens_hbm,
    routes_ref,
    mixing_ref,
    gate_hbm,
    up_hbm,
    down_hbm,
    mixed_ref,
    hess_hbm,
    tok,
    table,
    weight,
    gate_v,
    up_v,
    down_v,
    hid,
    part,
    in_b,
    in_a,
    in_z,
    hess_v,
    local_sem,
    tok_send,
    tok_recv,
    tab_send,
    tab_recv,
    pair_send,
    pair_recv,
    hid_send,
    hid_recv,
    back_send,
    back_recv,
    chain_send,
):
    groups = side * side
    rows, width = mixed_ref.shape
    half = gate_v.shape[2]
    me = lax.axis_index("expert")
    core = lax.axis_index("token")
    z, y, x = me // groups, (me // side) % side, me % side
    stride_a = jnp.where(core == 0, side, 1)
    stride_b = jnp.where(core == 0, 1, side)
    pos_a = jnp.where(core == 0, y, x)
    pos_b = jnp.where(core == 0, x, y)

    def peer_z(step):
        return me + ((z + step) % layers - z) * groups

    def peer_a(step):
        return me + ((pos_a + step) % side - pos_a) * stride_a

    def peer_b(step):
        return me + ((pos_b + step) % side - pos_b) * stride_b

    def slot(dz, da, db):
        return (da * stride_a + db * stride_b) * layers + dz

    def label(dz, da, db):
        return (da * side + db) * layers + dz

    def remote(src, dst, send, recv, to, to_core=None):
        return pltpu.make_async_remote_copy(
            src_ref=src,
            dst_ref=dst,
            send_sem=send,
            recv_sem=recv,
            device_id=(to, core if to_core is None else to_core),
            device_id_type=MESH,
        )

    def forward(dz, da, db):
        if db:
            source, to = slot(dz, da, 0), peer_b(db)
        elif da:
            source, to = slot(dz, 0, 0), peer_a(da)
        else:
            source, to = slot(0, 0, 0), peer_z(dz)
        name = label(dz, da, db)
        here = slot(dz, da, db)
        return (
            remote(table.at[source], table.at[here], tab_send.at[name], tab_recv.at[name], to),
            remote(
                tok.at[core, source],
                tok.at[core, here],
                tok_send.at[name],
                tok_recv.at[name],
                to,
            ),
        )

    def start(copies):
        for copy in copies:
            copy.start()

    def arrive(copies):
        for copy in copies:
            copy.wait_recv()

    def across(where):
        return remote(
            tok.at[core, where],
            tok.at[core, where],
            pair_send.at[where],
            pair_recv.at[where],
            me,
            1 - core,
        )

    def from_pair(where):
        return remote(
            tok.at[1 - core, where],
            tok.at[1 - core, where],
            pair_send.at[where],
            pair_recv.at[where],
            me,
            1 - core,
        )

    loads = [
        pltpu.make_async_copy(tokens_hbm, tok.at[core, 0], local_sem.at[0]),
        pltpu.make_async_copy(gate_hbm, gate_v, local_sem.at[1]),
        pltpu.make_async_copy(up_hbm, up_v, local_sem.at[2]),
        pltpu.make_async_copy(down_hbm, down_v, local_sem.at[3]),
    ]
    start(loads)
    barrier = pltpu.get_barrier_semaphore()
    partners = [(peer_z(d), core) for d in range(1, layers)]
    partners += [(peer_a(d), core) for d in range(1, side)]
    partners += [(peer_b(d), core) for d in range(1, side)]
    partners += [(me, 1 - core)]
    for partner in partners:
        pl.semaphore_signal(barrier, inc=1, device_id=partner, device_id_type=MESH)
    named = lax.broadcasted_iota(jnp.int32, (table.shape[1], rows), 0)
    shares = jnp.zeros((table.shape[1], rows), jnp.float32)
    for k in range(routes_ref.shape[0]):
        shares += jnp.where(routes_ref[k : k + 1, :] == named, mixing_ref[k : k + 1, :], 0.0)
    table[0, :, 0:rows] = shares
    loads[0].wait()
    pl.semaphore_wait(barrier, len(partners))

    orders = [
        sorted(range(1, layers), key=lambda d: (d if d <= place else layers - d, d))
        for place in range(layers)
    ]

    def coming(k):
        return sum(jnp.where(z == place, orders[place][k], 0) for place in range(layers))

    def chain(s, way, here):
        source = slot(s, 0, 0)
        there = slot(here, 0, 0)
        to = me + (groups if way == 0 else -groups)
        return (
            remote(
                table.at[source],
                table.at[there],
                chain_send.at[2 + way, s],
                tab_recv.at[here],
                to,
            ),
            remote(
                tok.at[core, source],
                tok.at[core, there],
                chain_send.at[way, s],
                tok_recv.at[here],
                to,
            ),
        )

    def along(s, act):
        @pl.when((z < layers - 1) & (s <= z))
        def _():
            for copy in chain(s, 0, s + 1):
                act(copy)

        @pl.when((z > 0) & ((s == 0) | (s > z)))
        def _():
            for copy in chain(s, 1, (s + layers - 1) % layers):
                act(copy)

    def spread(dz):
        along(dz, lambda copy: copy.start())
        for d in range(1, side):
            start(forward(dz, d, 0))
            start(forward(dz, 0, d))
        across(slot(dz, 0, 0)).start()

    def turn(dz):
        for da in range(1, side):
            arrive(forward(dz, da, 0))
            for db in range(1, side):
                start(forward(dz, da, db))
            across(slot(dz, da, 0)).start()

    def straight(dz):
        for db in range(1, side):
            arrive(forward(dz, 0, db))
            across(slot(dz, 0, db)).start()

    def last(dz):
        for da in range(1, side):
            for db in range(1, side):
                arrive(forward(dz, da, db))
                across(slot(dz, da, db)).start()

    sequence = [0] + [coming(k) for k in range(layers - 1)]
    spread(sequence[0])
    for k in range(1, layers):
        arrive(forward(sequence[k], 0, 0))
        spread(sequence[k])
        turn(sequence[k - 1])
        straight(sequence[k - 1])
    turn(sequence[-1])

    tall = layers * rows
    tile = min(256, half)
    diagonal = lax.broadcasted_iota(jnp.int32, (rows, rows), 0) == lax.broadcasted_iota(
        jnp.int32, (rows, rows), 1
    )

    def up_project(g):
        first = g * layers
        span = pl.ds(first, layers)
        for i in range(layers):
            from_pair(first + i).wait_recv()
            mine = table[first + i, pl.ds(me, 1), 0:rows]
            column = jnp.sum(jnp.where(diagonal, mine, 0.0), axis=1, keepdims=True)
            weight[first + i] = jnp.broadcast_to(column, weight.shape[1:])

        @pl.loop(0, half // tile)
        def _(j):
            cols = pl.ds(pl.multiple_of(j * tile, tile), tile)
            left = tok[0, span].reshape(tall, width)
            right = tok[1, span].reshape(tall, width)
            gate = jnp.dot(left, gate_v[0, :, cols], preferred_element_type=jnp.float32)
            gate += jnp.dot(right, gate_v[1, :, cols], preferred_element_type=jnp.float32)
            upper = jnp.dot(left, up_v[0, :, cols], preferred_element_type=jnp.float32)
            upper += jnp.dot(right, up_v[1, :, cols], preferred_element_type=jnp.float32)
            chosen = weight[span].reshape(tall, weight.shape[2])[:, 0:1] > 0
            value = gate / (1.0 + jnp.exp(-gate)) * upper
            value = jnp.where(chosen, value, 0.0).astype(jnp.bfloat16)
            hid[core, span, :, cols] = value.reshape(layers, rows, tile)

        hidden_copy(g).start()

    def hidden_copy(g):
        span = pl.ds(g * layers, layers)
        return remote(
            hid.at[core, span],
            hid.at[core, span],
            hid_send.at[g],
            hid_recv.at[g],
            me,
            1 - core,
        )

    def hidden_from_pair(g):
        span = pl.ds(g * layers, layers)
        return remote(
            hid.at[1 - core, span],
            hid.at[1 - core, span],
            hid_send.at[g],
            hid_recv.at[g],
            me,
            1 - core,
        )

    def down_project(g):
        span = pl.ds(g * layers, layers)
        hidden_from_pair(g).wait_recv()

        @pl.loop(0, width // tile)
        def _(j):
            cols = pl.ds(pl.multiple_of(j * tile, tile), tile)
            left = hid[0, span].reshape(tall, half)
            right = hid[1, span].reshape(tall, half)
            out = jnp.dot(left, down_v[0, :, cols], preferred_element_type=jnp.float32)
            out += jnp.dot(right, down_v[1, :, cols], preferred_element_type=jnp.float32)
            out *= weight[span].reshape(tall, weight.shape[2])[:, 0:1]
            part[span, :, cols] = out.astype(jnp.bfloat16).reshape(layers, rows, tile)

    def back(dz, da, db):
        name = label(dz, da, db)
        source = part.at[slot(dz, da, db)]
        if db:
            target, to = in_b.at[db - 1, da * layers + dz], peer_b(side - db)
        elif da:
            target, to = in_a.at[da - 1, dz], peer_a(side - da)
        else:
            target, to = in_z.at[dz - 1], peer_z(layers - dz)
        return remote(source, target, back_send.at[name], back_recv.at[name], to)

    def summed(dz, da):
        total = part[slot(dz, da, 0)].astype(jnp.float32)
        for db in range(1, side):
            back(dz, da, db).wait_recv()
            total += in_b[db - 1, da * layers + dz].astype(jnp.float32)
        if da == 0:
            for d in range(1, side):
                back(dz, d, 0).wait_recv()
                total += in_a[d - 1, dz].astype(jnp.float32)
        return total

    def send_back(da, db):
        for dz in range(layers):
            back(dz, da, db).start()

    for load in loads[1:]:
        load.wait()
    up_project(0)
    straight(sequence[-1])
    edge = [g for g in range(1, groups) if g // side == 0 or g % side == 0]
    for g in edge[:-1]:
        up_project(g)
    for k in range(layers // 2):
        last(sequence[k])
    up_project(edge[-1])
    for k in range(layers // 2, layers):
        last(sequence[k])
    for db in range(1, side):
        down_project(db * stride_b)
        send_back(0, db)
    inner = [g for g in range(1, groups) if g not in edge]
    for g in inner:
        up_project(g)
    for da in range(1, side):
        down_project(da * stride_a)
    for da in range(1, side):
        for db in range(1, side):
            down_project(da * stride_a + db * stride_b)
            send_back(da, db)
    down_project(0)

    named_rows = jnp.zeros((rows, weight.shape[2]), jnp.float32)
    for s in range(weight.shape[0]):
        named_rows += (weight[s] > 0).astype(jnp.float32)
    count = jnp.sum(named_rows, axis=0, keepdims=True)[:, 0:1]
    scale = 2.0 / count
    every = weight.shape[0] * rows
    for h in range(2):

        @pl.loop(0, half // tile)
        def _(j):
            cols = pl.ds(pl.multiple_of(j * tile, tile), tile)
            gram = lax.dot_general(
                hid[core, :, :, cols].reshape(every, tile),
                hid[h].reshape(every, half),
                (((0,), (0,)), ((), ())),
                preferred_element_type=jnp.float32,
            )
            hess_v[cols, pl.ds(h * half, half)] = gram * scale

    store = pltpu.make_async_copy(hess_v, hess_hbm, local_sem.at[0])
    store.start()

    far = sorted(range(1, layers), key=lambda d: -min(d, layers - d))
    for da in range(1, side):
        for dz in far + [0]:
            part[slot(dz, da, 0)] = summed(dz, da).astype(jnp.bfloat16)
            back(dz, da, 0).start()
    for dz in far:
        part[dz] = summed(dz, 0).astype(jnp.bfloat16)
        back(dz, 0, 0).start()
    total = summed(0, 0)
    for dz in range(1, layers):
        back(dz, 0, 0).wait_recv()
        total += in_z[dz - 1].astype(jnp.float32)
    mixed_ref[...] = total.astype(jnp.bfloat16)

    store.wait()
    for da in range(side):
        for db in range(side):
            for dz in range(layers):
                across(slot(dz, da, db)).wait_send()
                if da or db:
                    for copy in forward(dz, da, db):
                        copy.wait_send()
                if dz or da or db:
                    back(dz, da, db).wait_send()
    for dz in range(layers):
        along(dz, lambda copy: copy.wait_send())
    for g in range(groups):
        hidden_copy(g).wait_send()


def settle(mixed_in, hess_in, mixed_out, hess_out, mixed_v, hess_v, sems):
    pieces = 4
    span = hess_in.shape[0] // pieces
    moves = [(mixed_in, mixed_v, mixed_out)]
    for i in range(pieces):
        moves.append([ref.at[pl.ds(i * span, span)] for ref in (hess_in, hess_v, hess_out)])
    comes = [pltpu.make_async_copy(m[0], m[1], sems.at[0, i]) for i, m in enumerate(moves)]
    goes = [pltpu.make_async_copy(m[1], m[2], sems.at[1, i]) for i, m in enumerate(moves)]
    for copy in comes:
        copy.start()
    for come, go in zip(comes, goes):
        come.wait()
        go.start()
    for go in goes:
        go.wait()


def gathered(tokens, routes, mixing, gate_weight, up_weight, down_weight):
    count = lax.axis_size("expert")
    side = math.isqrt(count // 4)
    layers = count // (side * side)
    rows, width = tokens.shape
    depth, half = gate_weight.shape[1:]
    lanes = -(-rows // 128) * 128
    bf16, f32 = jnp.bfloat16, jnp.float32
    dma = pltpu.SemaphoreType.DMA
    hbm = pl.BlockSpec(memory_space=pl.ANY)
    vmem = pl.BlockSpec(memory_space=pltpu.VMEM)
    flops = 2 * count * rows * (2 * depth * half + 2 * half * width + 2 * half * half)
    mixed, hessian = pl.pallas_call(
        functools.partial(exchange, side, layers),
        out_shape=(
            jax.ShapeDtypeStruct((rows, width), bf16),
            jax.ShapeDtypeStruct((half, 2 * half), f32),
        ),
        in_specs=[hbm, vmem, vmem, hbm, hbm, hbm],
        out_specs=(vmem, hbm),
        scratch_shapes=[
            pltpu.VMEM((2, count, rows, width), bf16),
            pltpu.VMEM((count, count, lanes), f32),
            pltpu.VMEM((count, rows, 128), f32),
            pltpu.VMEM((2, width, half), bf16),
            pltpu.VMEM((2, width, half), bf16),
            pltpu.VMEM((2, half, width), bf16),
            pltpu.VMEM((2, count, rows, half), bf16),
            pltpu.VMEM((count, rows, width), bf16),
            pltpu.VMEM((side - 1, side * layers, rows, width), bf16),
            pltpu.VMEM((side - 1, layers, rows, width), bf16),
            pltpu.VMEM((layers - 1, rows, width), bf16),
            pltpu.VMEM((half, 2 * half), f32),
            dma((4,)),
            dma((count,)),
            dma((count,)),
            dma((count,)),
            dma((count,)),
            dma((count,)),
            dma((count,)),
            dma((side * side,)),
            dma((side * side,)),
            dma((count,)),
            dma((count,)),
            dma((4, layers)),
        ],
        compiler_params=pltpu.CompilerParams(
            collective_id=0, has_side_effects=True, vmem_limit_bytes=60 * 2**20
        ),
        cost_estimate=pl.CostEstimate(
            flops=flops,
            bytes_accessed=2 * (2 * depth * half + 2 * half * width),
            transcendentals=count * rows * half,
        ),
    )(
        tokens,
        routes.T,
        mixing.T,
        gate_weight.reshape(2, width, half),
        up_weight.reshape(2, width, half),
        down_weight.reshape(2, half, width),
    )
    mixed, hessian = pl.pallas_call(
        settle,
        out_shape=(
            jax.ShapeDtypeStruct(mixed.shape, bf16),
            jax.ShapeDtypeStruct(hessian.shape, f32),
        ),
        in_specs=[hbm, hbm],
        out_specs=(hbm, hbm),
        scratch_shapes=[
            pltpu.VMEM(mixed.shape, bf16),
            pltpu.VMEM(hessian.shape, f32),
            dma((2, 5)),
        ],
        compiler_params=pltpu.CompilerParams(vmem_limit_bytes=60 * 2**20),
    )(mixed, hessian)
    return (mixed, hessian[None])


def shards(tokens, routes, mixing, gate_weight, up_weight, down_weight):
    expert_count = lax.axis_size("expert")
    if 2 * routes.shape[1] >= expert_count:
        return gathered(tokens, routes, mixing, gate_weight, up_weight, down_weight)
    return dispatch(tokens, routes, mixing, gate_weight, up_weight, down_weight)


def solution(mesh):
    placed = (
        P("expert", "token"),
        P("expert", None),
        P("expert", None),
        P("expert", None, "token"),
        P("expert", None, "token"),
        P("expert", None, "token"),
    )
    return jax.shard_map(
        shards,
        mesh=mesh,
        in_specs=placed,
        out_specs=(P("expert", "token"), P("expert", "token", None)),
        check_vma=False,
    )
```

```python
import functools
import math

import jax
import jax.numpy as jnp
from jax import lax
from jax.experimental import pallas as pl
from jax.experimental.pallas import tpu as pltpu
from jax.sharding import PartitionSpec as P

MESH = pl.DeviceIdType.MESH


def dispatch(tokens, routes, mixing, gate_weight, up_weight, down_weight):
    tok_rows = tokens.shape[0]
    feat_width = tokens.shape[1]
    top_count = routes.shape[1]
    expert_count = lax.axis_size("expert")
    capacity = 2 * tok_rows * top_count // expert_count
    slot_total = expert_count * capacity
    flat_ids = routes.reshape(-1)
    chosen = (flat_ids[:, None] == jnp.arange(expert_count, dtype=jnp.int32)[None, :]).astype(
        jnp.int32
    )
    ranks = jnp.cumsum(chosen, axis=0) - chosen
    slots = jnp.sum(ranks * chosen, axis=1)
    counts = jnp.sum(chosen, axis=0)
    target = flat_ids * capacity + slots
    placing = (target[:, None] == jnp.arange(slot_total, dtype=jnp.int32)[None, :]).astype(
        jnp.bfloat16
    )
    placing = jnp.sum(placing.reshape(tok_rows, top_count, slot_total), axis=1)
    outgoing = lax.dot_general(
        placing, tokens, (((0,), (0,)), ((), ())), preferred_element_type=jnp.float32
    )
    outgoing = outgoing.astype(jnp.bfloat16).reshape(expert_count, capacity, feat_width)
    received, got_counts = (
        lax.all_to_all(outgoing, "expert", split_axis=0, concat_axis=0, tiled=True),
        lax.all_to_all(
            counts.astype(jnp.bfloat16), "expert", split_axis=0, concat_axis=0, tiled=True
        ),
    )
    rows_in = received.reshape(slot_total, feat_width)
    row_total = jnp.sum(got_counts.astype(jnp.float32))
    gate_local = gate_weight[0]
    up_local = up_weight[0]
    piece = lax.all_gather(rows_in, "token", axis=1, tiled=True)
    gate = jnp.dot(piece, gate_local, preferred_element_type=jnp.float32)
    upper = jnp.dot(piece, up_local, preferred_element_type=jnp.float32)
    hidden = (jax.nn.silu(gate) * upper).astype(jnp.bfloat16)
    down_local = down_weight[0]
    piece = lax.all_gather(hidden, "token", axis=1, tiled=True)
    out_sum = jnp.dot(piece, down_local, preferred_element_type=jnp.float32)
    outer = lax.dot_general(
        hidden, piece, (((0,), (0,)), ((), ())), preferred_element_type=jnp.float32
    )
    gram = outer
    out_sum, gram = (out_sum, gram)
    hessian = (2.0 / row_total * gram)[None]
    expert_out = out_sum.astype(jnp.bfloat16).reshape(expert_count, capacity, feat_width)
    returned = lax.all_to_all(expert_out, "expert", split_axis=0, concat_axis=0, tiled=True)
    picked = returned.reshape(slot_total, feat_width)[target]
    picked = picked.reshape(tok_rows, top_count, feat_width).astype(jnp.float32)
    mixed = jnp.sum(picked * mixing[:, :, None], axis=1).astype(jnp.bfloat16)
    return (mixed, hessian)


def exchange(
    side,
    layers,
    tokens_hbm,
    routes_ref,
    mixing_ref,
    gate_hbm,
    up_hbm,
    down_hbm,
    mixed_ref,
    hess_hbm,
    tok,
    table,
    weight,
    gate_v,
    up_v,
    down_v,
    hid,
    part,
    in_b,
    in_a,
    in_z,
    hess_v,
    local_sem,
    tok_send,
    tok_recv,
    tab_send,
    tab_recv,
    pair_send,
    pair_recv,
    hid_send,
    hid_recv,
    back_send,
    back_recv,
    chain_send,
):
    groups = side * side
    rows, width = mixed_ref.shape
    half = gate_v.shape[2]
    me = lax.axis_index("expert")
    core = lax.axis_index("token")
    z, y, x = me // groups, (me // side) % side, me % side
    stride_a = jnp.where(core == 0, side, 1)
    stride_b = jnp.where(core == 0, 1, side)
    pos_a = jnp.where(core == 0, y, x)
    pos_b = jnp.where(core == 0, x, y)

    def peer_z(step):
        return me + ((z + step) % layers - z) * groups

    def peer_a(step):
        return me + ((pos_a + step) % side - pos_a) * stride_a

    def peer_b(step):
        return me + ((pos_b + step) % side - pos_b) * stride_b

    def slot(dz, da, db):
        return (da * stride_a + db * stride_b) * layers + dz

    def label(dz, da, db):
        return (da * side + db) * layers + dz

    def remote(src, dst, send, recv, to, to_core=None):
        return pltpu.make_async_remote_copy(
            src_ref=src,
            dst_ref=dst,
            send_sem=send,
            recv_sem=recv,
            device_id=(to, core if to_core is None else to_core),
            device_id_type=MESH,
        )

    def forward(dz, da, db):
        if db:
            source, to = slot(dz, da, 0), peer_b(db)
        elif da:
            source, to = slot(dz, 0, 0), peer_a(da)
        else:
            source, to = slot(0, 0, 0), peer_z(dz)
        name = label(dz, da, db)
        here = slot(dz, da, db)
        return (
            remote(table.at[source], table.at[here], tab_send.at[name], tab_recv.at[name], to),
            remote(
                tok.at[core, source],
                tok.at[core, here],
                tok_send.at[name],
                tok_recv.at[name],
                to,
            ),
        )

    def start(copies):
        for copy in copies:
            copy.start()

    def arrive(copies):
        for copy in copies:
            copy.wait_recv()

    def across(where):
        return remote(
            tok.at[core, where],
            tok.at[core, where],
            pair_send.at[where],
            pair_recv.at[where],
            me,
            1 - core,
        )

    def from_pair(where):
        return remote(
            tok.at[1 - core, where],
            tok.at[1 - core, where],
            pair_send.at[where],
            pair_recv.at[where],
            me,
            1 - core,
        )

    loads = [
        pltpu.make_async_copy(tokens_hbm, tok.at[core, 0], local_sem.at[0]),
        pltpu.make_async_copy(gate_hbm, gate_v, local_sem.at[1]),
        pltpu.make_async_copy(up_hbm, up_v, local_sem.at[2]),
        pltpu.make_async_copy(down_hbm, down_v, local_sem.at[3]),
    ]
    start(loads)
    barrier = pltpu.get_barrier_semaphore()
    partners = [(peer_z(d), core) for d in range(1, layers)]
    partners += [(peer_a(d), core) for d in range(1, side)]
    partners += [(peer_b(d), core) for d in range(1, side)]
    partners += [(me, 1 - core)]
    for partner in partners:
        pl.semaphore_signal(barrier, inc=1, device_id=partner, device_id_type=MESH)
    named = lax.broadcasted_iota(jnp.int32, (table.shape[1], rows), 0)
    shares = jnp.zeros((table.shape[1], rows), jnp.float32)
    for k in range(routes_ref.shape[0]):
        shares += jnp.where(routes_ref[k : k + 1, :] == named, mixing_ref[k : k + 1, :], 0.0)
    table[0, :, 0:rows] = shares
    loads[0].wait()
    pl.semaphore_wait(barrier, len(partners))

    orders = [
        sorted(range(1, layers), key=lambda d: (d if d <= place else layers - d, d))
        for place in range(layers)
    ]

    def coming(k):
        return sum(jnp.where(z == place, orders[place][k], 0) for place in range(layers))

    def chain(s, way, here):
        source = slot(s, 0, 0)
        there = slot(here, 0, 0)
        to = me + (groups if way == 0 else -groups)
        return (
            remote(
                table.at[source],
                table.at[there],
                chain_send.at[2 + way, s],
                tab_recv.at[here],
                to,
            ),
            remote(
                tok.at[core, source],
                tok.at[core, there],
                chain_send.at[way, s],
                tok_recv.at[here],
                to,
            ),
        )

    def along(s, act):
        @pl.when((z < layers - 1) & (s <= z))
        def _():
            for copy in chain(s, 0, s + 1):
                act(copy)

        @pl.when((z > 0) & ((s == 0) | (s > z)))
        def _():
            for copy in chain(s, 1, (s + layers - 1) % layers):
                act(copy)

    def spread(dz):
        along(dz, lambda copy: copy.start())
        for d in range(1, side):
            start(forward(dz, d, 0))
            start(forward(dz, 0, d))
        across(slot(dz, 0, 0)).start()

    def turn(dz):
        for da in range(1, side):
            arrive(forward(dz, da, 0))
            for db in range(1, side):
                start(forward(dz, da, db))
            across(slot(dz, da, 0)).start()

    def straight(dz):
        for db in range(1, side):
            arrive(forward(dz, 0, db))
            across(slot(dz, 0, db)).start()

    def last(dz):
        for da in range(1, side):
            for db in range(1, side):
                arrive(forward(dz, da, db))
                across(slot(dz, da, db)).start()

    sequence = [0] + [coming(k) for k in range(layers - 1)]
    spread(sequence[0])
    for k in range(1, layers):
        arrive(forward(sequence[k], 0, 0))
        spread(sequence[k])
        turn(sequence[k - 1])
        straight(sequence[k - 1])
    turn(sequence[-1])

    tall = layers * rows
    tile = min(256, half)
    diagonal = lax.broadcasted_iota(jnp.int32, (rows, rows), 0) == lax.broadcasted_iota(
        jnp.int32, (rows, rows), 1
    )

    def up_project(g):
        first = g * layers
        span = pl.ds(first, layers)
        for i in range(layers):
            from_pair(first + i).wait_recv()
            mine = table[first + i, pl.ds(me, 1), 0:rows]
            column = jnp.sum(jnp.where(diagonal, mine, 0.0), axis=1, keepdims=True)
            weight[first + i] = jnp.broadcast_to(column, weight.shape[1:])

        @pl.loop(0, half // tile)
        def _(j):
            cols = pl.ds(pl.multiple_of(j * tile, tile), tile)
            left = tok[0, span].reshape(tall, width)
            right = tok[1, span].reshape(tall, width)
            gate = jnp.dot(left, gate_v[0, :, cols], preferred_element_type=jnp.float32)
            gate += jnp.dot(right, gate_v[1, :, cols], preferred_element_type=jnp.float32)
            upper = jnp.dot(left, up_v[0, :, cols], preferred_element_type=jnp.float32)
            upper += jnp.dot(right, up_v[1, :, cols], preferred_element_type=jnp.float32)
            chosen = weight[span].reshape(tall, weight.shape[2])[:, 0:1] > 0
            value = gate / (1.0 + jnp.exp(-gate)) * upper
            value = jnp.where(chosen, value, 0.0).astype(jnp.bfloat16)
            hid[core, span, :, cols] = value.reshape(layers, rows, tile)

        hidden_copy(g).start()

    def hidden_copy(g):
        span = pl.ds(g * layers, layers)
        return remote(
            hid.at[core, span],
            hid.at[core, span],
            hid_send.at[g],
            hid_recv.at[g],
            me,
            1 - core,
        )

    def hidden_from_pair(g):
        span = pl.ds(g * layers, layers)
        return remote(
            hid.at[1 - core, span],
            hid.at[1 - core, span],
            hid_send.at[g],
            hid_recv.at[g],
            me,
            1 - core,
        )

    def down_project(g):
        span = pl.ds(g * layers, layers)
        hidden_from_pair(g).wait_recv()

        @pl.loop(0, width // tile)
        def _(j):
            cols = pl.ds(pl.multiple_of(j * tile, tile), tile)
            left = hid[0, span].reshape(tall, half)
            right = hid[1, span].reshape(tall, half)
            out = jnp.dot(left, down_v[0, :, cols], preferred_element_type=jnp.float32)
            out += jnp.dot(right, down_v[1, :, cols], preferred_element_type=jnp.float32)
            out *= weight[span].reshape(tall, weight.shape[2])[:, 0:1]
            part[span, :, cols] = out.astype(jnp.bfloat16).reshape(layers, rows, tile)

    def back(dz, da, db):
        name = label(dz, da, db)
        source = part.at[slot(dz, da, db)]
        if db:
            target, to = in_b.at[db - 1, da * layers + dz], peer_b(side - db)
        elif da:
            target, to = in_a.at[da - 1, dz], peer_a(side - da)
        else:
            target, to = in_z.at[dz - 1], peer_z(layers - dz)
        return remote(source, target, back_send.at[name], back_recv.at[name], to)

    def summed(dz, da):
        total = part[slot(dz, da, 0)].astype(jnp.float32)
        for db in range(1, side):
            back(dz, da, db).wait_recv()
            total += in_b[db - 1, da * layers + dz].astype(jnp.float32)
        if da == 0:
            for d in range(1, side):
                back(dz, d, 0).wait_recv()
                total += in_a[d - 1, dz].astype(jnp.float32)
        return total

    def send_back(da, db):
        for dz in [*range(2, layers), 1, 0]:
            back(dz, da, db).start()

    for load in loads[1:]:
        load.wait()
    up_project(0)
    straight(sequence[-1])
    edge = [g for g in range(1, groups) if g // side == 0 or g % side == 0]
    for g in edge[:-1]:
        up_project(g)
    for k in range(layers // 2):
        last(sequence[k])
    up_project(edge[-1])
    for k in range(layers // 2, layers):
        last(sequence[k])
    for db in range(1, side):
        down_project(db * stride_b)
        send_back(0, db)
    inner = [g for g in range(1, groups) if g not in edge]
    for g in inner:
        up_project(g)
    for da in range(1, side):
        down_project(da * stride_a)
    for da in range(1, side):
        for db in range(1, side):
            down_project(da * stride_a + db * stride_b)
            send_back(da, db)
    down_project(0)

    named_rows = jnp.zeros((rows, weight.shape[2]), jnp.float32)
    for s in range(weight.shape[0]):
        named_rows += (weight[s] > 0).astype(jnp.float32)
    count = jnp.sum(named_rows, axis=0, keepdims=True)[:, 0:1]
    scale = 2.0 / count
    every = weight.shape[0] * rows
    for h in range(2):

        @pl.loop(0, half // tile)
        def _(j):
            cols = pl.ds(pl.multiple_of(j * tile, tile), tile)
            gram = lax.dot_general(
                hid[core, :, :, cols].reshape(every, tile),
                hid[h].reshape(every, half),
                (((0,), (0,)), ((), ())),
                preferred_element_type=jnp.float32,
            )
            hess_v[cols, pl.ds(h * half, half)] = gram * scale

    store = pltpu.make_async_copy(hess_v, hess_hbm, local_sem.at[0])
    store.start()

    far = sorted(range(1, layers), key=lambda d: -min(d, layers - d))
    for da in range(1, side):
        for dz in far + [0]:
            part[slot(dz, da, 0)] = summed(dz, da).astype(jnp.bfloat16)
            back(dz, da, 0).start()
    for dz in far:
        part[dz] = summed(dz, 0).astype(jnp.bfloat16)
        back(dz, 0, 0).start()
    total = summed(0, 0)
    for dz in range(1, layers):
        back(dz, 0, 0).wait_recv()
        total += in_z[dz - 1].astype(jnp.float32)
    mixed_ref[...] = total.astype(jnp.bfloat16)

    store.wait()
    for da in range(side):
        for db in range(side):
            for dz in range(layers):
                across(slot(dz, da, db)).wait_send()
                if da or db:
                    for copy in forward(dz, da, db):
                        copy.wait_send()
                if dz or da or db:
                    back(dz, da, db).wait_send()
    for dz in range(layers):
        along(dz, lambda copy: copy.wait_send())
    for g in range(groups):
        hidden_copy(g).wait_send()


def settle(mixed_in, hess_in, mixed_out, hess_out, mixed_v, hess_v, sems):
    pieces = 4
    span = hess_in.shape[0] // pieces
    moves = [(mixed_in, mixed_v, mixed_out)]
    for i in range(pieces):
        moves.append([ref.at[pl.ds(i * span, span)] for ref in (hess_in, hess_v, hess_out)])
    comes = [pltpu.make_async_copy(m[0], m[1], sems.at[0, i]) for i, m in enumerate(moves)]
    goes = [pltpu.make_async_copy(m[1], m[2], sems.at[1, i]) for i, m in enumerate(moves)]
    for copy in comes:
        copy.start()
    for come, go in zip(comes, goes):
        come.wait()
        go.start()
    for go in goes:
        go.wait()


def gathered(tokens, routes, mixing, gate_weight, up_weight, down_weight):
    count = lax.axis_size("expert")
    side = math.isqrt(count // 4)
    layers = count // (side * side)
    rows, width = tokens.shape
    depth, half = gate_weight.shape[1:]
    lanes = -(-rows // 128) * 128
    bf16, f32 = jnp.bfloat16, jnp.float32
    dma = pltpu.SemaphoreType.DMA
    hbm = pl.BlockSpec(memory_space=pl.ANY)
    vmem = pl.BlockSpec(memory_space=pltpu.VMEM)
    flops = 2 * count * rows * (2 * depth * half + 2 * half * width + 2 * half * half)
    mixed, hessian = pl.pallas_call(
        functools.partial(exchange, side, layers),
        out_shape=(
            jax.ShapeDtypeStruct((rows, width), bf16),
            jax.ShapeDtypeStruct((half, 2 * half), f32),
        ),
        in_specs=[hbm, vmem, vmem, hbm, hbm, hbm],
        out_specs=(vmem, hbm),
        scratch_shapes=[
            pltpu.VMEM((2, count, rows, width), bf16),
            pltpu.VMEM((count, count, lanes), f32),
            pltpu.VMEM((count, rows, 128), f32),
            pltpu.VMEM((2, width, half), bf16),
            pltpu.VMEM((2, width, half), bf16),
            pltpu.VMEM((2, half, width), bf16),
            pltpu.VMEM((2, count, rows, half), bf16),
            pltpu.VMEM((count, rows, width), bf16),
            pltpu.VMEM((side - 1, side * layers, rows, width), bf16),
            pltpu.VMEM((side - 1, layers, rows, width), bf16),
            pltpu.VMEM((layers - 1, rows, width), bf16),
            pltpu.VMEM((half, 2 * half), f32),
            dma((4,)),
            dma((count,)),
            dma((count,)),
            dma((count,)),
            dma((count,)),
            dma((count,)),
            dma((count,)),
            dma((side * side,)),
            dma((side * side,)),
            dma((count,)),
            dma((count,)),
            dma((4, layers)),
        ],
        compiler_params=pltpu.CompilerParams(
            collective_id=0, has_side_effects=True, vmem_limit_bytes=60 * 2**20
        ),
        cost_estimate=pl.CostEstimate(
            flops=flops,
            bytes_accessed=2 * (2 * depth * half + 2 * half * width),
            transcendentals=count * rows * half,
        ),
    )(
        tokens,
        routes.T,
        mixing.T,
        gate_weight.reshape(2, width, half),
        up_weight.reshape(2, width, half),
        down_weight.reshape(2, half, width),
    )
    mixed, hessian = pl.pallas_call(
        settle,
        out_shape=(
            jax.ShapeDtypeStruct(mixed.shape, bf16),
            jax.ShapeDtypeStruct(hessian.shape, f32),
        ),
        in_specs=[hbm, hbm],
        out_specs=(hbm, hbm),
        scratch_shapes=[
            pltpu.VMEM(mixed.shape, bf16),
            pltpu.VMEM(hessian.shape, f32),
            dma((2, 5)),
        ],
        compiler_params=pltpu.CompilerParams(vmem_limit_bytes=60 * 2**20),
    )(mixed, hessian)
    return (mixed, hessian[None])


def shards(tokens, routes, mixing, gate_weight, up_weight, down_weight):
    expert_count = lax.axis_size("expert")
    if 2 * routes.shape[1] >= expert_count:
        return gathered(tokens, routes, mixing, gate_weight, up_weight, down_weight)
    return dispatch(tokens, routes, mixing, gate_weight, up_weight, down_weight)


def solution(mesh):
    placed = (
        P("expert", "token"),
        P("expert", None),
        P("expert", None),
        P("expert", None, "token"),
        P("expert", None, "token"),
        P("expert", None, "token"),
    )
    return jax.shard_map(
        shards,
        mesh=mesh,
        in_specs=placed,
        out_specs=(P("expert", "token"), P("expert", "token", None)),
        check_vma=False,
    )
```
